32 devices in a mesh: groups: 2 (over y), region: 4 (over x, core), sub: 4 (over z).
Axes of the slice: x: 2, y: 2, z: 4, core: 2. Of those that a mesh axis runs over, the one named last changes fastest.
Arguments:
- node_latents: bfloat16 [4096, 512], P(('groups', 'region', 'sub')), parts along dimension 0, may hold values from -6 to 6
- edge_latents: bfloat16 [24576, 512], P(('groups', 'region', 'sub')), parts along dimension 0, may hold values from -6 to 6
- coarse_latents: bfloat16 [64, 512], P(('groups', 'region', 'sub')), parts along dimension 0, may hold values from -6 to 6
- node_cotangent: bfloat16 [4096, 512], P(('groups', 'region', 'sub')), parts along dimension 0, may hold values from -6 to 6
- edge_cotangent: bfloat16 [24576, 512], P(('groups', 'region', 'sub')), parts along dimension 0, may hold values from -6 to 6
- coarse_cotangent: bfloat16 [64, 512], P(('groups', 'region', 'sub')), parts along dimension 0, may hold values from -6 to 6
- edge_inner: bfloat16 [1536, 512], replicated, may hold values from -0.15625 to 0.15625
- edge_inner_bias: float32 [512], replicated, may hold values from -3 to 3
- edge_outer: bfloat16 [512, 512], replicated, may hold values from -0.25 to 0.25
- edge_outer_bias: float32 [512], replicated, may hold values from -3 to 3
- edge_gain: float32 [512], replicated, may hold values from 0.1 to 1.9
- node_inner: bfloat16 [1024, 512], replicated, may hold values from -0.1875 to 0.1875
- node_inner_bias: float32 [512], replicated, may hold values from -3 to 3
- node_outer: bfloat16 [512, 512], replicated, may hold values from -0.25 to 0.25
- node_outer_bias: float32 [512], replicated, may hold values from -3 to 3
- node_gain: float32 [512], replicated, may hold values from 0.1 to 1.9
- send_list: int32 [32, 8, 24], P(('groups', 'region', 'sub')), parts along dimension 0, may hold values from 0 to 127
- edge_sender: int32 [24576], P(('groups', 'region', 'sub')), parts along dimension 0, may hold values from 0 to 319
- edge_receiver: int32 [24576], P(('groups', 'region', 'sub')), parts along dimension 0, may hold values from 0 to 127
- coarse_sender: int32 [64], P('groups'), parts along dimension 0, may hold values from 0 to 15
- coarse_receiver: int32 [64], P('groups'), parts along dimension 0, may hold values from 0 to 15
Outputs:
- grad_nodes: bfloat16 [4096, 512], P(('groups', 'region', 'sub')), parts along dimension 0
- grad_edges: bfloat16 [24576, 512], P(('groups', 'region', 'sub')), parts along dimension 0
- grad_coarse: bfloat16 [64, 512], P(('groups', 'region', 'sub')), parts along dimension 0
- grad_edge_inner: float32 [3072, 512], P(('groups', 'region', 'sub')), parts along dimension 0
- grad_edge_outer: float32 [1024, 512], P(('groups', 'region', 'sub')), parts along dimension 0
- grad_node_inner: float32 [2048, 512], P(('groups', 'region', 'sub')), parts along dimension 0
- grad_node_outer: float32 [1024, 512], P(('groups', 'region', 'sub')), parts along dimension 0
The draws below stay inside these ranges and needn't reach their ends.
There are 2 independent parts, one for each index of `groups`. The reference program is written for one: setup_inputs(seed, part) draws one part's arguments, and reference() takes and returns one part's arrays. A program takes and returns all parts, laid end to end along the dimension named above; an argument that names none is the same for every part. Nothing has to cross between parts.
Inputs may be any that keep to these rules, and one draw needn't show every extreme that they name: send_list[p, m, j] is a row of device p, sent to its neighbour at offset m as that neighbour's j-th row from it. `edge_sender`: below 128: a row of the edge's own device; 128 + m * 24 + j: the j-th row sent to it by its neighbour at the opposite of offset m. `edge_receiver`: a row of the edge's own device. `coarse_sender`: coarse node c is the first row of device c. `coarse_receiver`: numbered as coarse_sender.
All inputs are finite; a program needn't handle non-finite values.
Results may differ from the reference program's by a relative error of at most 0.0076.
Values may be sent and summed in bfloat16 or wider, within the bound.
A program may use at most 128 MiB of HBM per device.

```python
import jax
import jax.numpy as jnp
from jax import lax

D = 512
NODE_DEV = 128
NEIGH = 8
HALO = 24
EDGE_DEV = 768
DEVS = 16
NODES = 2048
EDGES = 12288
EXT = 320
COARSE = 16
CEDGES = 32
N_REGION = 4
N_SUB = 4


def set_ends(values, stream_key, smallest, largest):
    extent = values.shape
    place = [jax.random.randint(jax.random.fold_in(stream_key, axis), (), 0, extent[axis]) for axis in range(len(extent))]
    values = values.at[tuple(place)].set(smallest)
    longest = extent.index(max(extent))
    place[longest] = (place[longest] + 1) % extent[longest]
    return values.at[tuple(place)].set(largest)


def shard_levels(own_key, shape, cuts, smallest, high):
    level, own = 1.0, jax.random.fold_in(own_key, 6)
    for axis_at, shards_of in cuts:
        heights = jnp.exp(jax.random.uniform(jax.random.fold_in(own, axis_at), (shards_of,), jnp.float32, smallest / len(cuts), high / len(cuts)))
        level = level * jnp.repeat(heights, shape[axis_at] // shards_of).reshape([-1 if axis == axis_at else 1 for axis in range(len(shape))])
    return level


def noise(stream_key, shape, deviation, most, shards=(), held_as=jnp.bfloat16):
    drawn = deviation * jax.random.normal(stream_key, shape, jnp.float32)
    if shards:
        drawn = drawn * shard_levels(stream_key, shape, shards, -0.22, 0.18)
    return jnp.clip(drawn, -most, most).astype(held_as)


def setup_inputs(seed: int = 0, part: int = 0) -> dict:
    arg_keys = jax.random.split(jax.random.key(seed), 22)
    part_splits = jax.random.split(jax.random.fold_in(arg_keys[21], part), 22)
    node_latents = noise(part_splits[0], (NODES, D), 1.0, 6.0, ((0, 16),))
    edge_latents = noise(part_splits[1], (EDGES, D), 1.0, 6.0, ((0, 16),))
    coarse_latents = noise(part_splits[2], (CEDGES, D), 1.0, 6.0, ((0, 16),))
    node_cotangent = noise(part_splits[3], (NODES, D), 1.0, 6.0, ((0, 16),))
    edge_cotangent = noise(part_splits[4], (EDGES, D), 1.0, 6.0, ((0, 16),))
    coarse_cotangent = noise(part_splits[5], (CEDGES, D), 1.0, 6.0, ((0, 16),))
    edge_inner = noise(arg_keys[6], (3 * D, D), (3 * D) ** -0.5, 0.15625)
    edge_inner_bias = noise(arg_keys[7], (D,), 0.5, 3.0, (), jnp.float32)
    edge_outer = noise(arg_keys[8], (D, D), D ** -0.5, 0.25)
    edge_outer_bias = noise(arg_keys[9], (D,), 0.5, 3.0, (), jnp.float32)
    edge_gain = jnp.clip(1.0 + 0.18 * jax.random.normal(arg_keys[10], (D,), jnp.float32), 0.1, 1.9)
    node_inner = noise(arg_keys[11], (2 * D, D), (2 * D) ** -0.5, 0.1875)
    node_inner_bias = noise(arg_keys[12], (D,), 0.5, 3.0, (), jnp.float32)
    node_outer = noise(arg_keys[13], (D, D), D ** -0.5, 0.25)
    node_outer_bias = noise(arg_keys[14], (D,), 0.5, 3.0, (), jnp.float32)
    node_gain = jnp.clip(1.0 + 0.18 * jax.random.normal(arg_keys[15], (D,), jnp.float32), 0.1, 1.9)
    send_list = set_ends(jax.random.randint(part_splits[16], (DEVS, NEIGH, HALO), 0, NODE_DEV), jax.random.fold_in(part_splits[16], 1), 0, NODE_DEV - 1).astype(jnp.int32)
    edge_sender = set_ends(jax.random.randint(part_splits[17], (EDGES,), 0, EXT), jax.random.fold_in(part_splits[17], 1), 0, EXT - 1).astype(jnp.int32)
    edge_receiver = set_ends(jax.random.randint(part_splits[18], (EDGES,), 0, NODE_DEV), jax.random.fold_in(part_splits[18], 1), 0, NODE_DEV - 1).astype(jnp.int32)
    coarse_sender = set_ends(jax.random.randint(part_splits[19], (CEDGES,), 0, COARSE), jax.random.fold_in(part_splits[19], 1), 0, COARSE - 1).astype(jnp.int32)
    coarse_receiver = set_ends(jax.random.randint(part_splits[20], (CEDGES,), 0, COARSE), jax.random.fold_in(part_splits[20], 1), 0, COARSE - 1).astype(jnp.int32)
    return dict(node_latents=node_latents, edge_latents=edge_latents, coarse_latents=coarse_latents, node_cotangent=node_cotangent, edge_cotangent=edge_cotangent, coarse_cotangent=coarse_cotangent, edge_inner=edge_inner, edge_inner_bias=edge_inner_bias, edge_outer=edge_outer, edge_outer_bias=edge_outer_bias, edge_gain=edge_gain, node_inner=node_inner, node_inner_bias=node_inner_bias, node_outer=node_outer, node_outer_bias=node_outer_bias, node_gain=node_gain, send_list=send_list, edge_sender=edge_sender, edge_receiver=edge_receiver, coarse_sender=coarse_sender, coarse_receiver=coarse_receiver)


def network_forward(inputs, inner, inner_bias, outer, outer_bias, gain):
    before = jnp.dot(inputs, inner, preferred_element_type=jnp.float32) + inner_bias
    hidden = jax.nn.silu(before).astype(jnp.bfloat16)
    after = jnp.dot(hidden, outer, preferred_element_type=jnp.float32) + outer_bias
    centred = after - lax.optimization_barrier(jnp.mean(after, axis=-1, keepdims=True))
    inv_scale = lax.rsqrt(lax.optimization_barrier(jnp.mean(centred * centred, axis=-1, keepdims=True)) + 1e-05)
    normed = centred * inv_scale
    return (normed * gain, (before, hidden, normed, inv_scale))

def contract_rows(left, right):
    return lax.dot_general(left, right, (((0,), (0,)), ((), ())), preferred_element_type=jnp.float32)

def contract_cols(left, right):
    return lax.dot_general(left, right, (((1,), (1,)), ((), ())), preferred_element_type=jnp.float32)

def network_backward(upstream, inputs, inner, outer, gain, stored):
    before, hidden, normed, inv_scale = stored
    scaled = upstream * gain
    grad_after = inv_scale * (scaled - lax.optimization_barrier(jnp.mean(scaled, axis=-1, keepdims=True)) - normed * lax.optimization_barrier(jnp.mean(scaled * normed, axis=-1, keepdims=True)))
    after_low = grad_after.astype(jnp.bfloat16)
    outer_grad = contract_rows(hidden, after_low)
    sigma = jax.nn.sigmoid(before)
    grad_before = contract_cols(after_low, outer) * sigma * (1.0 + before * (1.0 - sigma))
    before_low = grad_before.astype(jnp.bfloat16)
    inner_grad = contract_rows(inputs, before_low)
    input_grad = contract_cols(before_low, inner)
    return (input_grad, inner_grad, outer_grad)

def reference(node_latents, edge_latents, coarse_latents, node_cotangent, edge_cotangent, coarse_cotangent, edge_inner, edge_inner_bias, edge_outer, edge_outer_bias, edge_gain, node_inner, node_inner_bias, node_outer, node_outer_bias, node_gain, send_list, edge_sender, edge_receiver, coarse_sender, coarse_receiver):
    devices = N_REGION * N_SUB
    row_step = jnp.array([-1, -1, -1, 0, 0, 1, 1, 1], jnp.int32)
    col_step = jnp.array([-1, 0, 1, -1, 1, -1, 0, 1], jnp.int32)
    owner = (jnp.arange(EDGES) // EDGE_DEV).astype(jnp.int32)
    owner_row = (owner // N_SUB).astype(jnp.int32)
    owner_col = (owner % N_SUB).astype(jnp.int32)
    offset = jnp.maximum(edge_sender - NODE_DEV, 0).astype(jnp.int32)
    slot = (offset // HALO).astype(jnp.int32)
    source = ((owner_row - row_step[slot]) % N_REGION * N_SUB + (owner_col - col_step[slot]) % N_SUB).astype(jnp.int32)
    remote = send_list[source, slot, offset % HALO]
    senders = jnp.where(edge_sender < NODE_DEV, owner * NODE_DEV + edge_sender, source * NODE_DEV + remote).astype(jnp.int32)
    receivers = (owner * NODE_DEV + edge_receiver).astype(jnp.int32)
    coarse_from = (coarse_sender * NODE_DEV).astype(jnp.int32)
    coarse_to = (coarse_receiver * NODE_DEV).astype(jnp.int32)
    blocks = (edge_latents.reshape(devices, EDGE_DEV, D), senders.reshape(devices, EDGE_DEV), receivers.reshape(devices, EDGE_DEV), edge_cotangent.reshape(devices, EDGE_DEV, D))

    def edge_inputs(latents, from_rows, to_rows):
        return jnp.concatenate([latents, node_latents[from_rows], node_latents[to_rows]], axis=1)

    def forward_block(block):
        latents, from_rows, to_rows, unused = block
        message, stored = network_forward(edge_inputs(latents, from_rows, to_rows), edge_inner, edge_inner_bias, edge_outer, edge_outer_bias, edge_gain)
        return (latents.astype(jnp.float32) + message).astype(jnp.bfloat16)
    updated = lax.map(forward_block, blocks).reshape(EDGES, D)
    summed = jax.ops.segment_sum(updated.astype(jnp.float32), receivers, num_segments=NODES)
    coarse_inputs = jnp.concatenate([coarse_latents, node_latents[coarse_from], node_latents[coarse_to]], axis=1)
    coarse_message, coarse_stored = network_forward(coarse_inputs, edge_inner, edge_inner_bias, edge_outer, edge_outer_bias, edge_gain)
    coarse_updated = (coarse_latents.astype(jnp.float32) + coarse_message).astype(jnp.bfloat16)
    summed = summed + jax.ops.segment_sum(coarse_updated.astype(jnp.float32), coarse_to, num_segments=NODES)
    node_inputs = jnp.concatenate([node_latents, summed.astype(jnp.bfloat16)], axis=1)
    unused_out, node_stored = network_forward(node_inputs, node_inner, node_inner_bias, node_outer, node_outer_bias, node_gain)
    node_grad, node_inner_grad, node_outer_grad = network_backward(node_cotangent.astype(jnp.float32), node_inputs, node_inner, node_outer, node_gain, node_stored)
    grad_nodes = node_cotangent.astype(jnp.float32) + node_grad[:, :D]
    grad_summed = node_grad[:, D:]

    def backward_block(carry, block):
        latents, from_rows, to_rows, upstream = block
        inputs = edge_inputs(latents, from_rows, to_rows)
        message, stored = network_forward(inputs, edge_inner, edge_inner_bias, edge_outer, edge_outer_bias, edge_gain)
        total = upstream.astype(jnp.float32) + grad_summed[to_rows]
        input_grad, inner_grad, outer_grad = network_backward(total, inputs, edge_inner, edge_outer, edge_gain, stored)
        return ((carry[0] + inner_grad, carry[1] + outer_grad), ((total + input_grad[:, :D]).astype(jnp.bfloat16), input_grad[:, D:2 * D], input_grad[:, 2 * D:]))
    start = (jnp.zeros((3 * D, D), jnp.float32), jnp.zeros((D, D), jnp.float32))
    (inner_sum, outer_sum), (grad_edges, from_grads, to_grads) = lax.scan(backward_block, start, blocks)
    grad_nodes = grad_nodes + jax.ops.segment_sum(from_grads.reshape(EDGES, D), senders, num_segments=NODES)
    grad_nodes = grad_nodes + jax.ops.segment_sum(to_grads.reshape(EDGES, D), receivers, num_segments=NODES)
    coarse_total = coarse_cotangent.astype(jnp.float32) + grad_summed[coarse_to]
    coarse_grad, coarse_inner, coarse_outer = network_backward(coarse_total, coarse_inputs, edge_inner, edge_outer, edge_gain, coarse_stored)
    grad_coarse = (coarse_total + coarse_grad[:, :D]).astype(jnp.bfloat16)
    grad_nodes = grad_nodes + jax.ops.segment_sum(coarse_grad[:, D:2 * D], coarse_from, num_segments=NODES)
    grad_nodes = grad_nodes + jax.ops.segment_sum(coarse_grad[:, 2 * D:], coarse_to, num_segments=NODES)
    return (grad_nodes.astype(jnp.bfloat16), grad_edges.reshape(EDGES, D), grad_coarse, inner_sum + coarse_inner, outer_sum + coarse_outer, node_inner_grad, node_outer_grad)
```

```python
import jax
import jax.numpy as jnp
from jax import lax
from jax.experimental import pallas as pl
from jax.experimental.pallas import tpu as pltpu
from jax.sharding import PartitionSpec as P


def passed_along(value, axis, steps):
    count = lax.axis_size(axis)
    pairs = [(source, (source + steps) % count) for source in range(count)]
    return lax.ppermute(value, axis, pairs)


def for_sending(array):

    def short(part):
        return part.astype(jnp.bfloat16) if part.dtype == jnp.float32 else part

    return jax.tree.map(short, array)


def network_forward(inputs, inner, inner_bias, outer, outer_bias, gain):
    before = jnp.dot(inputs, inner, preferred_element_type=jnp.float32) + inner_bias
    hidden = jax.nn.silu(before).astype(jnp.bfloat16)
    after = jnp.dot(hidden, outer, preferred_element_type=jnp.float32) + outer_bias
    centred = after - jnp.mean(after, axis=-1, keepdims=True)
    inv_scale = lax.rsqrt(jnp.mean(centred * centred, axis=-1, keepdims=True) + 1e-05)
    normed = centred * inv_scale
    return (normed * gain, (before, hidden, normed, inv_scale))


def contract_rows(left, right):
    return lax.dot_general(
        left, right, (((0,), (0,)), ((), ())), preferred_element_type=jnp.float32
    )


def contract_cols(left, right):
    return lax.dot_general(
        left, right, (((1,), (1,)), ((), ())), preferred_element_type=jnp.float32
    )


def network_backward(upstream, inputs, inner, outer, gain, stored):
    before, hidden, normed, inv_scale = stored
    scaled = upstream * gain
    grad_after = inv_scale * (
        scaled
        - jnp.mean(scaled, axis=-1, keepdims=True)
        - normed * jnp.mean(scaled * normed, axis=-1, keepdims=True)
    )
    after_low = grad_after.astype(jnp.bfloat16)
    outer_grad = contract_rows(hidden, after_low)
    sigma = jax.nn.sigmoid(before)
    grad_before = contract_cols(after_low, outer) * sigma * (1.0 + before * (1.0 - sigma))
    before_low = grad_before.astype(jnp.bfloat16)
    inner_grad = contract_rows(inputs, before_low)
    input_grad = contract_cols(before_low, inner)
    return (input_grad, inner_grad, outer_grad)


def onehot_sum(targets, count, values):
    picker = (targets[None, :] == jnp.arange(count, dtype=jnp.int32)[:, None]).astype(jnp.float32)
    return jnp.dot(
        picker, values, preferred_element_type=jnp.float32, precision=lax.Precision.HIGHEST
    )


def with_centre(blocks):
    empty = jnp.zeros((1,) + blocks.shape[1:], blocks.dtype)
    grid = jnp.concatenate([blocks[:4], empty, blocks[4:]], axis=0)
    return grid.reshape((3, 3) + blocks.shape[1:])


def without_centre(grid):
    flat = grid.reshape((9,) + grid.shape[2:])
    return jnp.concatenate([flat[:4], flat[5:]], axis=0)


def per_device(
    node_latents,
    edge_latents,
    coarse_latents,
    node_cotangent,
    edge_cotangent,
    coarse_cotangent,
    edge_inner,
    edge_inner_bias,
    edge_outer,
    edge_outer_bias,
    edge_gain,
    node_inner,
    node_inner_bias,
    node_outer,
    node_outer_bias,
    node_gain,
    send_list,
    edge_sender,
    edge_receiver,
    coarse_sender,
    coarse_receiver,
):
    latent = node_latents.shape[1]
    local_rows = node_latents.shape[0]
    region_count = lax.axis_size("region")
    sub_count = lax.axis_size("sub")
    device_count = region_count * sub_count
    position = lax.axis_index(("region", "sub"))
    neighbours = send_list.shape[1]
    halo_rows = send_list.shape[2]
    send_rows = send_list[0].reshape(-1)
    outgoing = node_latents[send_rows].reshape(neighbours, halo_rows, latent)
    grid = with_centre(outgoing)
    region_moved = [passed_along(grid[step + 1], "region", step) for step in (-1, 1)]
    sectioned = jnp.stack([region_moved[0], grid[1], region_moved[1]], axis=0)
    sub_moved = [passed_along(sectioned[:, step + 1], "sub", step) for step in (-1, 1)]
    incoming = without_centre(jnp.stack([sub_moved[0], sectioned[:, 1], sub_moved[1]], axis=1))
    extended = jnp.concatenate(
        [node_latents, incoming.reshape(neighbours * halo_rows, latent)], axis=0
    )
    inputs = jnp.concatenate(
        [edge_latents, extended[edge_sender], node_latents[edge_receiver]], axis=1
    )
    message, edge_stored = network_forward(
        inputs, edge_inner, edge_inner_bias, edge_outer, edge_outer_bias, edge_gain
    )
    updated = (edge_latents.astype(jnp.float32) + message).astype(jnp.bfloat16)
    receive_low = (
        edge_receiver[None, :] == jnp.arange(local_rows, dtype=jnp.int32)[:, None]
    ).astype(jnp.bfloat16)
    summed = jnp.dot(receive_low, updated, preferred_element_type=jnp.float32)
    coarse_rows = 1
    coarse_edges = coarse_latents.shape[0]
    own_nodes = node_latents[:coarse_rows]
    coarse_nodes, coarse_edge_rows, coarse_upstream = (
        lax.all_gather(own_nodes, ("region", "sub"), axis=0, tiled=True),
        lax.all_gather(coarse_latents, ("region", "sub"), axis=0, tiled=True),
        lax.all_gather(coarse_cotangent, ("region", "sub"), axis=0, tiled=True),
    )
    coarse_inputs = jnp.concatenate(
        [coarse_edge_rows, coarse_nodes[coarse_sender], coarse_nodes[coarse_receiver]], axis=1
    )
    coarse_message, coarse_stored = network_forward(
        coarse_inputs, edge_inner, edge_inner_bias, edge_outer, edge_outer_bias, edge_gain
    )
    coarse_updated = (coarse_edge_rows.astype(jnp.float32) + coarse_message).astype(jnp.bfloat16)
    coarse_summed = jax.ops.segment_sum(
        coarse_updated.astype(jnp.float32), coarse_receiver, num_segments=device_count
    )
    coarse_own = lax.dynamic_slice_in_dim(coarse_summed, position * coarse_rows, coarse_rows)
    summed = summed.at[:coarse_rows].add(coarse_own)
    node_inputs = jnp.concatenate([node_latents, summed.astype(jnp.bfloat16)], axis=1)
    unused_out, node_stored = network_forward(
        node_inputs, node_inner, node_inner_bias, node_outer, node_outer_bias, node_gain
    )
    node_grad, node_inner_grad, node_outer_grad = network_backward(
        node_cotangent.astype(jnp.float32),
        node_inputs,
        node_inner,
        node_outer,
        node_gain,
        node_stored,
    )
    grad_nodes = node_cotangent.astype(jnp.float32) + node_grad[:, :latent]
    grad_summed = node_grad[:, latent:]
    total = edge_cotangent.astype(jnp.float32) + grad_summed[edge_receiver]
    edge_grad, fine_inner, fine_outer = network_backward(
        total, inputs, edge_inner, edge_outer, edge_gain, edge_stored
    )
    grad_edges = (total + edge_grad[:, :latent]).astype(jnp.bfloat16)
    extended_grads = onehot_sum(
        edge_sender, local_rows + neighbours * halo_rows, edge_grad[:, latent : 2 * latent]
    )
    grad_nodes = grad_nodes + extended_grads[:local_rows]
    grad_nodes = grad_nodes + onehot_sum(edge_receiver, local_rows, edge_grad[:, 2 * latent :])
    returning = extended_grads[local_rows:].reshape(neighbours, halo_rows, latent)
    back_grid = with_centre(returning)
    sub_back = [
        passed_along(back_grid[:, step + 1].astype(jnp.bfloat16), "sub", -step).astype(jnp.float32)
        for step in (-1, 1)
    ]
    sectioned_back = jnp.stack([sub_back[0], back_grid[:, 1], sub_back[1]], axis=1)
    region_back = [
        passed_along(for_sending(sectioned_back[step + 1]), "region", -step) for step in (-1, 1)
    ]
    returned = without_centre(
        jnp.stack([region_back[0], sectioned_back[1], region_back[1]], axis=0)
    )
    grad_nodes = grad_nodes + onehot_sum(
        send_rows, local_rows, returned.reshape(neighbours * halo_rows, latent)
    )
    coarse_needed = lax.all_gather(grad_summed[:coarse_rows], ("region", "sub"), axis=0, tiled=True)
    coarse_total = coarse_upstream.astype(jnp.float32) + coarse_needed[coarse_receiver]
    coarse_grad, coarse_inner, coarse_outer = network_backward(
        coarse_total, coarse_inputs, edge_inner, edge_outer, edge_gain, coarse_stored
    )
    coarse_edge_grads = (coarse_total + coarse_grad[:, :latent]).astype(jnp.bfloat16)
    coarse_node_grads = jax.ops.segment_sum(
        coarse_grad[:, latent : 2 * latent], coarse_sender, num_segments=device_count
    )
    coarse_node_grads = coarse_node_grads + jax.ops.segment_sum(
        coarse_grad[:, 2 * latent :], coarse_receiver, num_segments=device_count
    )
    grad_coarse = lax.dynamic_slice_in_dim(coarse_edge_grads, position * coarse_edges, coarse_edges)
    own_grads = lax.dynamic_slice_in_dim(coarse_node_grads, position * coarse_rows, coarse_rows)
    only_first = (position == 0).astype(jnp.float32)
    coarse_inner = coarse_inner * only_first
    coarse_outer = coarse_outer * only_first
    grad_nodes = grad_nodes.at[:coarse_rows].add(own_grads)
    weight_terms = (
        fine_inner + coarse_inner,
        fine_outer + coarse_outer,
        node_inner_grad,
        node_outer_grad,
    )
    reduced = (
        lax.psum_scatter(weight_terms[0], ("region", "sub"), scatter_dimension=0, tiled=True),
        lax.psum_scatter(weight_terms[1], ("region", "sub"), scatter_dimension=0, tiled=True),
        lax.psum_scatter(weight_terms[2], ("region", "sub"), scatter_dimension=0, tiled=True),
        lax.psum_scatter(weight_terms[3], ("region", "sub"), scatter_dimension=0, tiled=True),
    )
    return (
        grad_nodes.astype(jnp.bfloat16),
        grad_edges,
        grad_coarse,
        reduced[0],
        reduced[1],
        reduced[2],
        reduced[3],
    )


def dot(left, right):
    return jnp.dot(left, right, preferred_element_type=jnp.float32)


def one_hot(hits):
    return jnp.where(hits, 1.0, 0.0).astype(jnp.bfloat16)


def column_hot(row, first, count):
    tall = jnp.transpose(jnp.broadcast_to(row, (128, row.shape[1])))
    lanes = lax.broadcasted_iota(jnp.int32, tall.shape, 1)
    parts = [one_hot(tall == lanes + (first + at)) for at in range(0, count, 128)]
    return jnp.concatenate(parts, axis=1) if len(parts) > 1 else parts[0]


def row_hot(row, count):
    shape = (count, row.shape[1])
    rows = lax.broadcasted_iota(jnp.int32, shape, 0)
    return one_hot(jnp.broadcast_to(row, shape) == rows)


def two_parts(value):
    high = value.astype(jnp.bfloat16)
    return high, (value - high.astype(jnp.float32)).astype(jnp.bfloat16)


def layer_norm_parts(after):
    centred = after - jnp.mean(after, axis=-1, keepdims=True)
    inv_scale = lax.rsqrt(jnp.mean(centred * centred, axis=-1, keepdims=True) + 1e-05)
    return centred * inv_scale, inv_scale


def gradient_after(upstream, gain, normed, inv_scale):
    scaled = upstream * gain
    return inv_scale * (
        scaled
        - jnp.mean(scaled, axis=-1, keepdims=True)
        - normed * jnp.mean(scaled * normed, axis=-1, keepdims=True)
    )


OFFSETS = ((-1, -1), (-1, 0), (-1, 1), (0, -1), (0, 1), (1, -1), (1, 0), (1, 1))
SLOT = 32
SIDE = 4
DEVICES = SIDE * SIDE
FINE = 768
ROWS = 896
OWN = 128
EXTENDED = OWN + 8 * SLOT
PIECES = ((0, 256), (256, 256), (512, 256), (768, 128))
CHUNKS = ((96, 512), (32, 512), (96, 256), (96, 256))


def step_kernel(
    index_ref, params_ref, packet_ref,
    nodes_ref, edges_ref, node_cot_ref, edge_cot_ref,
    w1_ref, w2_ref, v1_ref, v2_ref,
    grad_nodes_ref, grad_edges_ref, grad_coarse_ref,
    out_ei_ref, out_eo_ref, out_ni_ref, out_no_ref,
    joined, ext, outgoing, coarse_tiles, before_ref, hidden_ref, normed_ref, inv_ref,
    updated_ref, after_low_ref, before_low_ref, masked, send_back, returned,
    coarse_cot, coarse_sums,
    g0, g1, g2, g3, a0, a1, a2, a3, b0, b1, b2, b3, c0, c1, c2, c3,
    t0, t1, t2, t3, d0, d1, d2, d3, e0, e1, e2, e3,
    halo_send, halo_recv, coarse_send, coarse_recv, sums_send, sums_recv,
    back_send, back_recv, s1_send, s1_recv, s2_send, s2_recv, s3_send, s3_recv,
):
    bf16, f32 = jnp.bfloat16, jnp.float32
    group = lax.axis_index("groups")
    region = lax.axis_index("region")
    sub = lax.axis_index("sub")
    position = region * SIDE + sub
    core = lax.rem(region, 2)
    column = lax.div(region, 2)

    def at(r, s):
        return (group, lax.rem(r + SIDE, SIDE), lax.rem(s + SIDE, SIDE))

    def flat(k):
        other = lax.rem(position + k + DEVICES, DEVICES)
        return other, (group, lax.div(other, SIDE), lax.rem(other, SIDE))

    def remote(src, dst, send, recv, device):
        return pltpu.make_async_remote_copy(
            src_ref=src, dst_ref=dst, send_sem=send, recv_sem=recv,
            device_id=device, device_id_type=pl.DeviceIdType.MESH,
        )

    barrier = pltpu.get_barrier_semaphore()
    for k in range(1, DEVICES):
        pl.semaphore_signal(
            barrier, inc=1, device_id=flat(k)[1], device_id_type=pl.DeviceIdType.MESH
        )
    nodes = nodes_ref[...]
    send_row = index_ref[:, 1792:2048]
    outgoing[...] = dot(column_hot(send_row, 0, OWN), nodes).astype(bf16)
    coarse_tiles[position] = packet_ref[...]
    ext[0:OWN, :] = nodes
    pl.semaphore_wait(barrier, DEVICES - 1)

    waits = []
    halo = []
    for m, (dr, ds) in enumerate(OFFSETS):
        slot = pl.ds(OWN + m * SLOT, SLOT)
        copy = remote(
            outgoing.at[pl.ds(m * SLOT, SLOT)], ext.at[slot],
            halo_send.at[m], halo_recv.at[m], at(region + dr, sub + ds),
        )
        copy.start()
        halo.append(copy)
    coarse = []
    for k in range(1, DEVICES):
        _, device = flat(k)
        sender, _ = flat(-k)
        remote(
            coarse_tiles.at[position], coarse_tiles.at[position],
            coarse_send.at[k], coarse_recv.at[k], device,
        ).start()
        coarse.append(remote(
            coarse_tiles.at[position], coarse_tiles.at[sender],
            coarse_send.at[k], coarse_recv.at[k], device,
        ))

    b1_row, b2_row, gain = params_ref[0:1, :], params_ref[1:2, :], params_ref[2:3, :]
    c1_row, c2_row, node_gain = params_ref[3:4, :], params_ref[4:5, :], params_ref[5:6, :]

    for first, size in PIECES[:3]:
        rows = pl.ds(first, size)
        joined[rows, 0:512] = edges_ref[rows, :]
        masked[rows, :] = edges_ref[rows, :]
        picker = column_hot(index_ref[:, 896 + first:896 + first + size], 0, OWN)
        joined[rows, 1024:1536] = dot(picker, nodes).astype(bf16)
    for copy in halo:
        copy.wait()
    extended = ext[...]
    for first, size in PIECES[:3]:
        rows = pl.ds(first, size)
        picker = column_hot(index_ref[:, first:first + size], 0, EXTENDED)
        joined[rows, 512:1024] = dot(picker, extended).astype(bf16)

    piece_rows = lax.broadcasted_iota(jnp.int32, (128, 1), 0)
    is_own = (piece_rows >= 2 * position) & (piece_rows < 2 * position + 2)
    own_mask = jnp.where(is_own, 1.0, 0.0)

    for first, size in PIECES:
        rows = pl.ds(first, size)
        if first == FINE:
            for copy in coarse:
                copy.wait()
            table = coarse_tiles[...].reshape(DEVICES * 16, 512)
            picked = dot(column_hot(index_ref[:, 2048:2176], 0, DEVICES * 16), table)
            blank = jnp.zeros((96, 512), f32)

            def placed(part):
                return jnp.concatenate([part, blank], axis=0)

            latents = placed(picked[0:32])
            joined[rows, 0:512] = latents.astype(bf16)
            joined[rows, 512:1024] = placed(picked[32:64]).astype(bf16)
            joined[rows, 1024:1536] = placed(picked[64:96]).astype(bf16)
            masked[rows, :] = (latents * own_mask).astype(bf16)
            coarse_cot[...] = placed(picked[96:128])
        before = dot(joined[rows, :], w1_ref[...]) + b1_row
        before_ref[rows, :] = before
        hidden = (before * jax.nn.sigmoid(before)).astype(bf16)
        hidden_ref[rows, :] = hidden
        after = dot(hidden, w2_ref[...]) + b2_row
        normed, inv_scale = layer_norm_parts(after)
        normed_ref[rows, :] = normed
        inv_ref[rows, :] = jnp.broadcast_to(inv_scale, (size, 128))
        updated_ref[rows, :] = (joined[rows, 0:512].astype(f32) + normed * gain).astype(bf16)
    coarse_rows = pl.ds(FINE, 128)
    hidden_ref[coarse_rows, :] = (hidden_ref[coarse_rows, :].astype(f32) * own_mask).astype(bf16)

    to_receiver = row_hot(index_ref[:, 896:1792], OWN)
    summed = dot(to_receiver, updated_ref[...])

    summed_low = summed.astype(bf16)
    node_before = dot(nodes, v1_ref[0:512, :]) + dot(summed_low, v1_ref[512:1024, :]) + c1_row
    sigma = jax.nn.sigmoid(node_before)
    node_hidden = (node_before * sigma).astype(bf16)
    node_normed, node_inv = layer_norm_parts(dot(node_hidden, v2_ref[...]) + c2_row)
    node_cot = node_cot_ref[...].astype(f32)
    node_after = gradient_after(node_cot, node_gain, node_normed, node_inv).astype(bf16)
    node_low = (
        contract_cols(node_after, v2_ref[...]) * sigma * (1.0 + node_before * (1.0 - sigma))
    ).astype(bf16)
    grad_summed = contract_cols(node_low, v1_ref[512:1024, :])
    for part in range(4):
        coarse_sums[position, part:part + 1, :] = grad_summed[0:1, 128 * part:128 * part + 128]
    sums = []
    for k in range(1, DEVICES):
        _, device = flat(k)
        sender, _ = flat(-k)
        remote(
            coarse_sums.at[position], coarse_sums.at[position],
            sums_send.at[k], sums_recv.at[k], device,
        ).start()
        sums.append(remote(
            coarse_sums.at[position], coarse_sums.at[sender],
            sums_send.at[k], sums_recv.at[k], device,
        ))

    grads, mine, passing, crossed = (g0, g1, g2, g3), (a0, a1, a2, a3), (b0, b1, b2, b3), (c0, c1, c2, c3)
    totals, along, arrived = (t0, t1, t2, t3), (d0, d1, d2, d3), (e0, e1, e2, e3)
    partner_core = (group, column * 2 + (1 - core), sub)
    partner_column = (group, (1 - column) * 2 + core, sub)

    def core_copy(n, which):
        return remote(
            grads[n].at[which * 2 + (1 - core)], mine[n].at[which],
            s1_send.at[n, which], s1_recv.at[n, which], partner_core,
        )

    def start_core(n):
        core_copy(n, 1 - column).start()
        core_copy(n, column).start()

    def column_copy(n):
        return remote(passing[n], crossed[n], s2_send.at[n], s2_recv.at[n], partner_column)

    def start_column(n):
        core_copy(n, 1 - column).wait()
        passing[n][...] = (
            grads[n][(1 - column) * 2 + core].astype(f32) + mine[n][1 - column].astype(f32)
        ).astype(bf16)
        column_copy(n).start()

    def total_column(n):
        core_copy(n, column).wait()
        column_copy(n).wait()
        totals[n][...] = (
            grads[n][column * 2 + core].astype(f32)
            + mine[n][column].astype(f32)
            + crossed[n][...].astype(f32)
        )

    def line_copy(n, way, block):
        step = 1 if way == 0 else SIDE - 1
        return remote(
            along[n].at[way, block], arrived[n].at[way, block],
            s3_send.at[n, way, block], s3_recv.at[n, way, block],
            (group, region, lax.rem(sub + step, SIDE)),
        )

    def line_step(n, k):
        for way, block, first, sends in (
            (0, 3 - k, 0, sub < 3 - k), (1, k, SIDE - 1, sub > k)
        ):
            @pl.when(sends & (sub == first))
            def _():
                along[n][way, block] = totals[n][block].astype(bf16)
                line_copy(n, way, block).start()

            @pl.when(sends & (sub != first))
            def _():
                line_copy(n, way, block).wait_recv()
                along[n][way, block] = (
                    totals[n][block] + arrived[n][way, block].astype(f32)
                ).astype(bf16)
                line_copy(n, way, block).start()

    def line_end(n):
        @pl.when(sub > 0)
        def _():
            line_copy(n, 0, sub).wait_recv()
            totals[n][sub] = totals[n][sub] + arrived[n][0, sub].astype(f32)

        @pl.when(sub < SIDE - 1)
        def _():
            line_copy(n, 1, sub).wait_recv()
            totals[n][sub] = totals[n][sub] + arrived[n][1, sub].astype(f32)

        for k in range(SIDE - 1):
            @pl.when(sub < 3 - k)
            def _():
                line_copy(n, 0, 3 - k).wait_send()

            @pl.when(sub > k)
            def _():
                line_copy(n, 1, k).wait_send()
        return totals[n][sub]

    node_inner_grad = jnp.concatenate(
        [contract_rows(nodes, node_low), contract_rows(summed_low, node_low)], axis=0
    ).astype(bf16)
    node_outer_grad = contract_rows(node_hidden, node_after).astype(bf16)
    g0[:, :, 0:64, :] = node_inner_grad.reshape(SIDE, SIDE, 64, 512)
    g0[:, :, 64:96, :] = node_outer_grad.reshape(SIDE, SIDE, 32, 512)
    start_core(0)
    node_direct = node_cot + contract_cols(node_low, v1_ref[0:512, :])

    sums_high, sums_low = two_parts(grad_summed)
    for first, size in PIECES:
        rows = pl.ds(first, size)
        if first == FINE:
            for copy in sums:
                copy.wait()
            gathered = jnp.concatenate([coarse_sums[:, part, :] for part in range(4)], axis=1)
            gathered = jnp.concatenate([gathered, jnp.zeros((OWN - DEVICES, 512), f32)], axis=0)
            high, low = two_parts(gathered)
            picker = column_hot(index_ref[:, 2176:2304], 0, OWN)
            total = coarse_cot[...] + (dot(picker, high) + dot(picker, low))
        else:
            picker = column_hot(index_ref[:, 896 + first:896 + first + size], 0, OWN)
            total = edge_cot_ref[rows, :].astype(f32) + (dot(picker, sums_high) + dot(picker, sums_low))
        after_low = gradient_after(
            total, gain, normed_ref[rows, :], inv_ref[rows, 0:1]
        ).astype(bf16)
        after_low_ref[rows, :] = after_low
        before = before_ref[rows, :]
        sigma = jax.nn.sigmoid(before)
        before_low = (
            contract_cols(after_low, w2_ref[...]) * sigma * (1.0 + before * (1.0 - sigma))
        ).astype(bf16)
        before_low_ref[rows, :] = before_low
        direct = total + contract_cols(before_low, w1_ref[0:512, :])
        if first == FINE:
            row_pair = [
                jnp.sum(jnp.where(piece_rows == 2 * position + j, direct, 0.0), axis=0, keepdims=True)
                for j in range(2)
            ]
            is_second = lax.broadcasted_iota(jnp.int32, (2, 512), 0) == 1
            grad_coarse_ref[...] = jnp.where(is_second, row_pair[1], row_pair[0]).astype(bf16)
        else:
            grad_edges_ref[rows, :] = direct.astype(bf16)
        if first == 256:
            start_column(0)

    g1[...] = contract_rows(hidden_ref[...], after_low_ref[...]).astype(bf16).reshape(g1.shape)
    start_core(1)
    to_sender = row_hot(index_ref[:, 0:896], EXTENDED)
    from_high, from_low = two_parts(dot(to_sender, before_low_ref[...]))
    to_high, to_low = two_parts(dot(to_receiver, before_low_ref[...]))
    w1b, w1c = w1_ref[512:1024, :], w1_ref[1024:1536, :]
    from_grads = contract_cols(from_high, w1b) + contract_cols(from_low, w1b)
    send_back[...] = from_grads[OWN:].astype(bf16)
    back = []
    for m, (dr, ds) in enumerate(OFFSETS):
        slot = pl.ds(m * SLOT, SLOT)
        copy = remote(
            send_back.at[slot], returned.at[slot],
            back_send.at[m], back_recv.at[m], at(region - dr, sub - ds),
        )
        copy.start()
        back.append(copy)
    start_column(1)
    for n, buffer in ((2, g2), (3, g3)):
        cols = slice(256 * (n - 2), 256 * (n - 2) + 256)
        inner = jnp.concatenate([
            contract_rows(masked[...], before_low_ref[:, cols]),
            contract_rows(extended, from_high[:, cols]) + contract_rows(extended, from_low[:, cols]),
            contract_rows(nodes, to_high[:, cols]) + contract_rows(nodes, to_low[:, cols]),
        ], axis=0)
        buffer[...] = inner.astype(bf16).reshape(buffer.shape)
        start_core(n)
        if n == 2:
            total_column(0)
            line_step(0, 0)
    start_column(2)
    line_step(0, 1)
    start_column(3)
    own = node_direct + from_grads[0:OWN]
    own = own + (contract_cols(to_high, w1c) + contract_cols(to_low, w1c))
    line_step(0, 2)
    for copy in back:
        copy.wait()
    own = own + dot(row_hot(send_row, OWN), returned[...])
    grad_nodes_ref[...] = own.astype(bf16)
    total_column(1)
    line_step(1, 0)
    line_step(1, 1)
    line_step(1, 2)
    total_column(2)
    line_step(2, 0)
    node_block = line_end(0)
    out_ni_ref[...] = node_block[0:64]
    out_no_ref[...] = node_block[64:96]
    line_step(2, 1)
    total_column(3)
    line_step(3, 0)
    line_step(2, 2)
    line_step(3, 1)
    out_eo_ref[...] = line_end(1)
    line_step(3, 2)
    out_ei_ref[:, 0:256] = line_end(2)
    out_ei_ref[:, 256:512] = line_end(3)


def fused_device(
    node_latents, edge_latents, coarse_latents, node_cotangent, edge_cotangent, coarse_cotangent,
    edge_inner, edge_inner_bias, edge_outer, edge_outer_bias, edge_gain,
    node_inner, node_inner_bias, node_outer, node_outer_bias, node_gain,
    send_list, edge_sender, edge_receiver, coarse_sender, coarse_receiver,
):
    bf16, f32, dma = jnp.bfloat16, jnp.float32, pltpu.SemaphoreType.DMA
    position = lax.axis_index("region") * SIDE + lax.axis_index("sub")
    halo_slot = jnp.maximum(edge_sender - OWN, 0) // send_list.shape[2]
    padded_sender = edge_sender + halo_slot * (SLOT - send_list.shape[2])
    none = jnp.full((96,), -1, jnp.int32)
    every = jnp.arange(2 * DEVICES, dtype=jnp.int32)
    tile_row = 16 * (every // 2) + every % 2
    index = jnp.concatenate([
        padded_sender, jnp.where(coarse_sender == position, 0, -1), none,
        edge_receiver, jnp.where(coarse_receiver == position, 0, -1), none,
        jnp.pad(send_list[0], ((0, 0), (0, SLOT - send_list.shape[2])), constant_values=-1).reshape(-1),
        tile_row + 1, 16 * coarse_sender, 16 * coarse_receiver, tile_row + 3,
        coarse_receiver, none,
    ]).reshape(1, -1)
    blank = jnp.zeros((512,), f32)
    params = jnp.stack([
        edge_inner_bias, edge_outer_bias, edge_gain,
        node_inner_bias, node_outer_bias, node_gain, blank, blank,
    ])
    packet = jnp.concatenate(
        [node_latents[:1], coarse_latents, coarse_cotangent, jnp.zeros((11, 512), bf16)], axis=0
    )

    def per_chunk(make):
        return [pltpu.VMEM(*make(rows, cols)) for rows, cols in CHUNKS]

    scratch = [
        pltpu.VMEM((ROWS, 1536), bf16),
        pltpu.VMEM((EXTENDED, 512), bf16),
        pltpu.VMEM((8 * SLOT, 512), bf16),
        pltpu.VMEM((DEVICES, 16, 512), bf16),
        pltpu.VMEM((ROWS, 512), f32),
        pltpu.VMEM((ROWS, 512), bf16),
        pltpu.VMEM((ROWS, 512), f32),
        pltpu.VMEM((ROWS, 128), f32),
        pltpu.VMEM((ROWS, 512), bf16),
        pltpu.VMEM((ROWS, 512), bf16),
        pltpu.VMEM((ROWS, 512), bf16),
        pltpu.VMEM((ROWS, 512), bf16),
        pltpu.VMEM((8 * SLOT, 512), bf16),
        pltpu.VMEM((8 * SLOT, 512), bf16),
        pltpu.VMEM((128, 512), f32),
        pltpu.VMEM((DEVICES, 4, 128), f32),
        *per_chunk(lambda n, c: ((SIDE, SIDE, n, c), bf16)),
        *per_chunk(lambda n, c: ((2, SIDE, n, c), bf16)),
        *per_chunk(lambda n, c: ((SIDE, n, c), bf16)),
        *per_chunk(lambda n, c: ((SIDE, n, c), bf16)),
        *per_chunk(lambda n, c: ((SIDE, n, c), f32)),
        *per_chunk(lambda n, c: ((2, SIDE, n, c), bf16)),
        *per_chunk(lambda n, c: ((2, SIDE, n, c), bf16)),
        dma((8,)), dma((8,)), dma((DEVICES,)), dma((DEVICES,)), dma((DEVICES,)), dma((DEVICES,)),
        dma((8,)), dma((8,)), dma((4, 2)), dma((4, 2)), dma((4,)), dma((4,)),
        dma((4, 2, SIDE)), dma((4, 2, SIDE)),
    ]
    shape = jax.ShapeDtypeStruct
    vmem = pl.BlockSpec(memory_space=pltpu.VMEM)
    return pl.pallas_call(
        step_kernel,
        out_shape=(
            shape((OWN, 512), bf16), shape((FINE, 512), bf16), shape((2, 512), bf16),
            shape((96, 512), f32), shape((32, 512), f32), shape((64, 512), f32), shape((32, 512), f32),
        ),
        in_specs=[vmem] * 11,
        out_specs=(vmem,) * 7,
        scratch_shapes=scratch,
        compiler_params=pltpu.CompilerParams(
            collective_id=0, has_side_effects=True, vmem_limit_bytes=58 * 2**20
        ),
    )(
        index, params, packet, node_latents, edge_latents, node_cotangent, edge_cotangent,
        edge_inner, edge_outer, node_inner, node_outer,
    )


def solution(mesh):
    in_specs = (
        P(("groups", "region", "sub"), None),
        P(("groups", "region", "sub"), None),
        P(("groups", "region", "sub"), None),
        P(("groups", "region", "sub"), None),
        P(("groups", "region", "sub"), None),
        P(("groups", "region", "sub"), None),
        P(),
        P(),
        P(),
        P(),
        P(),
        P(),
        P(),
        P(),
        P(),
        P(),
        P(("groups", "region", "sub"), None, None),
        P(("groups", "region", "sub")),
        P(("groups", "region", "sub")),
        P("groups"),
        P("groups"),
    )
    out_specs = (
        P(("groups", "region", "sub"), None),
        P(("groups", "region", "sub"), None),
        P(("groups", "region", "sub"), None),
        P(("groups", "region", "sub"), None),
        P(("groups", "region", "sub"), None),
        P(("groups", "region", "sub"), None),
        P(("groups", "region", "sub"), None),
    )
    small = mesh.shape["region"] == SIDE and mesh.shape["sub"] == SIDE
    return jax.shard_map(
        fused_device if small else per_device, mesh=mesh, in_specs=in_specs, out_specs=out_specs, check_vma=False
    )
```

```python
import jax
import jax.numpy as jnp
from jax import lax
from jax.experimental import pallas as pl
from jax.experimental.pallas import tpu as pltpu
from jax.sharding import PartitionSpec as P


def passed_along(value, axis, steps):
    count = lax.axis_size(axis)
    pairs = [(source, (source + steps) % count) for source in range(count)]
    return lax.ppermute(value, axis, pairs)


def for_sending(array):

    def short(part):
        return part.astype(jnp.bfloat16) if part.dtype == jnp.float32 else part

    return jax.tree.map(short, array)


def network_forward(inputs, inner, inner_bias, outer, outer_bias, gain):
    before = jnp.dot(inputs, inner, preferred_element_type=jnp.float32) + inner_bias
    hidden = jax.nn.silu(before).astype(jnp.bfloat16)
    after = jnp.dot(hidden, outer, preferred_element_type=jnp.float32) + outer_bias
    centred = after - jnp.mean(after, axis=-1, keepdims=True)
    inv_scale = lax.rsqrt(jnp.mean(centred * centred, axis=-1, keepdims=True) + 1e-05)
    normed = centred * inv_scale
    return (normed * gain, (before, hidden, normed, inv_scale))


def contract_rows(left, right):
    return lax.dot_general(
        left, right, (((0,), (0,)), ((), ())), preferred_element_type=jnp.float32
    )


def contract_cols(left, right):
    return lax.dot_general(
        left, right, (((1,), (1,)), ((), ())), preferred_element_type=jnp.float32
    )


def network_backward(upstream, inputs, inner, outer, gain, stored):
    before, hidden, normed, inv_scale = stored
    scaled = upstream * gain
    grad_after = inv_scale * (
        scaled
        - jnp.mean(scaled, axis=-1, keepdims=True)
        - normed * jnp.mean(scaled * normed, axis=-1, keepdims=True)
    )
    after_low = grad_after.astype(jnp.bfloat16)
    outer_grad = contract_rows(hidden, after_low)
    sigma = jax.nn.sigmoid(before)
    grad_before = contract_cols(after_low, outer) * sigma * (1.0 + before * (1.0 - sigma))
    before_low = grad_before.astype(jnp.bfloat16)
    inner_grad = contract_rows(inputs, before_low)
    input_grad = contract_cols(before_low, inner)
    return (input_grad, inner_grad, outer_grad)


def onehot_sum(targets, count, values):
    picker = (targets[None, :] == jnp.arange(count, dtype=jnp.int32)[:, None]).astype(jnp.float32)
    return jnp.dot(
        picker, values, preferred_element_type=jnp.float32, precision=lax.Precision.HIGHEST
    )


def with_centre(blocks):
    empty = jnp.zeros((1,) + blocks.shape[1:], blocks.dtype)
    grid = jnp.concatenate([blocks[:4], empty, blocks[4:]], axis=0)
    return grid.reshape((3, 3) + blocks.shape[1:])


def without_centre(grid):
    flat = grid.reshape((9,) + grid.shape[2:])
    return jnp.concatenate([flat[:4], flat[5:]], axis=0)


def per_device(
    node_latents,
    edge_latents,
    coarse_latents,
    node_cotangent,
    edge_cotangent,
    coarse_cotangent,
    edge_inner,
    edge_inner_bias,
    edge_outer,
    edge_outer_bias,
    edge_gain,
    node_inner,
    node_inner_bias,
    node_outer,
    node_outer_bias,
    node_gain,
    send_list,
    edge_sender,
    edge_receiver,
    coarse_sender,
    coarse_receiver,
):
    latent = node_latents.shape[1]
    local_rows = node_latents.shape[0]
    region_count = lax.axis_size("region")
    sub_count = lax.axis_size("sub")
    device_count = region_count * sub_count
    position = lax.axis_index(("region", "sub"))
    neighbours = send_list.shape[1]
    halo_rows = send_list.shape[2]
    send_rows = send_list[0].reshape(-1)
    outgoing = node_latents[send_rows].reshape(neighbours, halo_rows, latent)
    grid = with_centre(outgoing)
    region_moved = [passed_along(grid[step + 1], "region", step) for step in (-1, 1)]
    sectioned = jnp.stack([region_moved[0], grid[1], region_moved[1]], axis=0)
    sub_moved = [passed_along(sectioned[:, step + 1], "sub", step) for step in (-1, 1)]
    incoming = without_centre(jnp.stack([sub_moved[0], sectioned[:, 1], sub_moved[1]], axis=1))
    extended = jnp.concatenate(
        [node_latents, incoming.reshape(neighbours * halo_rows, latent)], axis=0
    )
    inputs = jnp.concatenate(
        [edge_latents, extended[edge_sender], node_latents[edge_receiver]], axis=1
    )
    message, edge_stored = network_forward(
        inputs, edge_inner, edge_inner_bias, edge_outer, edge_outer_bias, edge_gain
    )
    updated = (edge_latents.astype(jnp.float32) + message).astype(jnp.bfloat16)
    receive_low = (
        edge_receiver[None, :] == jnp.arange(local_rows, dtype=jnp.int32)[:, None]
    ).astype(jnp.bfloat16)
    summed = jnp.dot(receive_low, updated, preferred_element_type=jnp.float32)
    coarse_rows = 1
    coarse_edges = coarse_latents.shape[0]
    own_nodes = node_latents[:coarse_rows]
    coarse_nodes, coarse_edge_rows, coarse_upstream = (
        lax.all_gather(own_nodes, ("region", "sub"), axis=0, tiled=True),
        lax.all_gather(coarse_latents, ("region", "sub"), axis=0, tiled=True),
        lax.all_gather(coarse_cotangent, ("region", "sub"), axis=0, tiled=True),
    )
    coarse_inputs = jnp.concatenate(
        [coarse_edge_rows, coarse_nodes[coarse_sender], coarse_nodes[coarse_receiver]], axis=1
    )
    coarse_message, coarse_stored = network_forward(
        coarse_inputs, edge_inner, edge_inner_bias, edge_outer, edge_outer_bias, edge_gain
    )
    coarse_updated = (coarse_edge_rows.astype(jnp.float32) + coarse_message).astype(jnp.bfloat16)
    coarse_summed = jax.ops.segment_sum(
        coarse_updated.astype(jnp.float32), coarse_receiver, num_segments=device_count
    )
    coarse_own = lax.dynamic_slice_in_dim(coarse_summed, position * coarse_rows, coarse_rows)
    summed = summed.at[:coarse_rows].add(coarse_own)
    node_inputs = jnp.concatenate([node_latents, summed.astype(jnp.bfloat16)], axis=1)
    unused_out, node_stored = network_forward(
        node_inputs, node_inner, node_inner_bias, node_outer, node_outer_bias, node_gain
    )
    node_grad, node_inner_grad, node_outer_grad = network_backward(
        node_cotangent.astype(jnp.float32),
        node_inputs,
        node_inner,
        node_outer,
        node_gain,
        node_stored,
    )
    grad_nodes = node_cotangent.astype(jnp.float32) + node_grad[:, :latent]
    grad_summed = node_grad[:, latent:]
    total = edge_cotangent.astype(jnp.float32) + grad_summed[edge_receiver]
    edge_grad, fine_inner, fine_outer = network_backward(
        total, inputs, edge_inner, edge_outer, edge_gain, edge_stored
    )
    grad_edges = (total + edge_grad[:, :latent]).astype(jnp.bfloat16)
    extended_grads = onehot_sum(
        edge_sender, local_rows + neighbours * halo_rows, edge_grad[:, latent : 2 * latent]
    )
    grad_nodes = grad_nodes + extended_grads[:local_rows]
    grad_nodes = grad_nodes + onehot_sum(edge_receiver, local_rows, edge_grad[:, 2 * latent :])
    returning = extended_grads[local_rows:].reshape(neighbours, halo_rows, latent)
    back_grid = with_centre(returning)
    sub_back = [
        passed_along(back_grid[:, step + 1].astype(jnp.bfloat16), "sub", -step).astype(jnp.float32)
        for step in (-1, 1)
    ]
    sectioned_back = jnp.stack([sub_back[0], back_grid[:, 1], sub_back[1]], axis=1)
    region_back = [
        passed_along(for_sending(sectioned_back[step + 1]), "region", -step) for step in (-1, 1)
    ]
    returned = without_centre(
        jnp.stack([region_back[0], sectioned_back[1], region_back[1]], axis=0)
    )
    grad_nodes = grad_nodes + onehot_sum(
        send_rows, local_rows, returned.reshape(neighbours * halo_rows, latent)
    )
    coarse_needed = lax.all_gather(grad_summed[:coarse_rows], ("region", "sub"), axis=0, tiled=True)
    coarse_total = coarse_upstream.astype(jnp.float32) + coarse_needed[coarse_receiver]
    coarse_grad, coarse_inner, coarse_outer = network_backward(
        coarse_total, coarse_inputs, edge_inner, edge_outer, edge_gain, coarse_stored
    )
    coarse_edge_grads = (coarse_total + coarse_grad[:, :latent]).astype(jnp.bfloat16)
    coarse_node_grads = jax.ops.segment_sum(
        coarse_grad[:, latent : 2 * latent], coarse_sender, num_segments=device_count
    )
    coarse_node_grads = coarse_node_grads + jax.ops.segment_sum(
        coarse_grad[:, 2 * latent :], coarse_receiver, num_segments=device_count
    )
    grad_coarse = lax.dynamic_slice_in_dim(coarse_edge_grads, position * coarse_edges, coarse_edges)
    own_grads = lax.dynamic_slice_in_dim(coarse_node_grads, position * coarse_rows, coarse_rows)
    only_first = (position == 0).astype(jnp.float32)
    coarse_inner = coarse_inner * only_first
    coarse_outer = coarse_outer * only_first
    grad_nodes = grad_nodes.at[:coarse_rows].add(own_grads)
    weight_terms = (
        fine_inner + coarse_inner,
        fine_outer + coarse_outer,
        node_inner_grad,
        node_outer_grad,
    )
    reduced = (
        lax.psum_scatter(weight_terms[0], ("region", "sub"), scatter_dimension=0, tiled=True),
        lax.psum_scatter(weight_terms[1], ("region", "sub"), scatter_dimension=0, tiled=True),
        lax.psum_scatter(weight_terms[2], ("region", "sub"), scatter_dimension=0, tiled=True),
        lax.psum_scatter(weight_terms[3], ("region", "sub"), scatter_dimension=0, tiled=True),
    )
    return (
        grad_nodes.astype(jnp.bfloat16),
        grad_edges,
        grad_coarse,
        reduced[0],
        reduced[1],
        reduced[2],
        reduced[3],
    )


def dot(left, right):
    return jnp.dot(left, right, preferred_element_type=jnp.float32)


def one_hot(hits):
    return jnp.where(hits, 1.0, 0.0).astype(jnp.bfloat16)


def column_hot(row, first, count):
    tall = jnp.transpose(jnp.broadcast_to(row, (128, row.shape[1])))
    lanes = lax.broadcasted_iota(jnp.int32, tall.shape, 1)
    parts = [one_hot(tall == lanes + (first + at)) for at in range(0, count, 128)]
    return jnp.concatenate(parts, axis=1) if len(parts) > 1 else parts[0]


def row_hot(row, count):
    shape = (count, row.shape[1])
    rows = lax.broadcasted_iota(jnp.int32, shape, 0)
    return one_hot(jnp.broadcast_to(row, shape) == rows)


def two_parts(value):
    high = value.astype(jnp.bfloat16)
    return high, (value - high.astype(jnp.float32)).astype(jnp.bfloat16)


def layer_norm_parts(after):
    centred = after - jnp.mean(after, axis=-1, keepdims=True)
    inv_scale = lax.rsqrt(jnp.mean(centred * centred, axis=-1, keepdims=True) + 1e-05)
    return centred * inv_scale, inv_scale


def gradient_after(upstream, gain, normed, inv_scale):
    scaled = upstream * gain
    return inv_scale * (
        scaled
        - jnp.mean(scaled, axis=-1, keepdims=True)
        - normed * jnp.mean(scaled * normed, axis=-1, keepdims=True)
    )


OFFSETS = ((-1, -1), (-1, 0), (-1, 1), (0, -1), (0, 1), (1, -1), (1, 0), (1, 1))
SLOT = 32
SIDE = 4
DEVICES = SIDE * SIDE
FINE = 768
ROWS = 896
OWN = 128
EXTENDED = OWN + 8 * SLOT
PIECES = ((0, 256), (256, 256), (512, 256), (768, 128))
CHUNKS = ((96, 512), (32, 512), (96, 256), (96, 256))


def step_kernel(
    index_ref, params_ref, packet_ref,
    nodes_ref, edges_hbm, node_cot_ref, edge_cot_hbm, w1_hbm, w2_hbm, v1_hbm, v2_hbm,
    grad_nodes_ref, grad_edges_ref, grad_coarse_ref,
    out_ei_ref, out_eo_ref, out_ni_ref, out_no_ref,
    edges_ref, edge_cot_ref, w1_ref, w2_ref, v1_ref, v2_ref, load_sems,
    joined, ext, outgoing, coarse_tiles, before_ref, hidden_ref, normed_ref, inv_ref,
    updated_ref, after_low_ref, before_low_ref, masked, send_back, returned,
    coarse_cot, coarse_sums,
    g0, g1, g2, g3, a0, a1, a2, a3, b0, b1, b2, b3, c0, c1, c2, c3,
    t0, t1, t2, t3, d0, d1, d2, d3, e0, e1, e2, e3,
    halo_send, halo_recv, coarse_send, coarse_recv, sums_send, sums_recv,
    back_send, back_recv, s1_send, s1_recv, s2_send, s2_recv, s3_send, s3_recv,
):
    bf16, f32 = jnp.bfloat16, jnp.float32
    group = lax.axis_index("groups")
    region = lax.axis_index("region")
    sub = lax.axis_index("sub")
    position = region * SIDE + sub
    core = lax.rem(region, 2)
    column = lax.div(region, 2)

    def at(r, s):
        return (group, lax.rem(r + SIDE, SIDE), lax.rem(s + SIDE, SIDE))

    def flat(k):
        other = lax.rem(position + k + DEVICES, DEVICES)
        return other, (group, lax.div(other, SIDE), lax.rem(other, SIDE))

    def remote(src, dst, send, recv, device):
        return pltpu.make_async_remote_copy(
            src_ref=src, dst_ref=dst, send_sem=send, recv_sem=recv,
            device_id=device, device_id_type=pl.DeviceIdType.MESH,
        )

    loads = [
        pltpu.make_async_copy(src, dst, load_sems.at[n])
        for n, (src, dst) in enumerate((
            (edges_hbm, edges_ref), (w1_hbm, w1_ref), (w2_hbm, w2_ref),
            (v1_hbm, v1_ref), (v2_hbm, v2_ref), (edge_cot_hbm, edge_cot_ref),
        ))
    ]
    barrier = pltpu.get_barrier_semaphore()
    for k in range(1, DEVICES):
        pl.semaphore_signal(
            barrier, inc=1, device_id=flat(k)[1], device_id_type=pl.DeviceIdType.MESH
        )
    for load in loads:
        load.start()
    nodes = nodes_ref[...]
    send_row = index_ref[:, 1792:2048]
    outgoing[...] = dot(column_hot(send_row, 0, OWN), nodes).astype(bf16)
    coarse_tiles[position] = packet_ref[...]
    ext[0:OWN, :] = nodes
    pl.semaphore_wait(barrier, DEVICES - 1)

    waits = []
    halo = []
    for m, (dr, ds) in enumerate(OFFSETS):
        slot = pl.ds(OWN + m * SLOT, SLOT)
        copy = remote(
            outgoing.at[pl.ds(m * SLOT, SLOT)], ext.at[slot],
            halo_send.at[m], halo_recv.at[m], at(region + dr, sub + ds),
        )
        copy.start()
        halo.append(copy)
    coarse = []
    for k in range(1, DEVICES):
        _, device = flat(k)
        sender, _ = flat(-k)
        remote(
            coarse_tiles.at[position], coarse_tiles.at[position],
            coarse_send.at[k], coarse_recv.at[k], device,
        ).start()
        coarse.append(remote(
            coarse_tiles.at[position], coarse_tiles.at[sender],
            coarse_send.at[k], coarse_recv.at[k], device,
        ))

    b1_row, b2_row, gain = params_ref[0:1, :], params_ref[1:2, :], params_ref[2:3, :]
    c1_row, c2_row, node_gain = params_ref[3:4, :], params_ref[4:5, :], params_ref[5:6, :]

    loads[0].wait()
    loads[1].wait()
    for first, size in PIECES[:3]:
        rows = pl.ds(first, size)
        masked[rows, :] = edges_ref[rows, :]
        picker = column_hot(index_ref[:, 896 + first:896 + first + size], 0, OWN)
        to_rows = dot(picker, nodes).astype(bf16)
        before_ref[rows, :] = (
            dot(edges_ref[rows, :], w1_ref[0:512, :]) + dot(to_rows, w1_ref[1024:1536, :]) + b1_row
        )
    loads[2].wait()
    for copy in halo:
        copy.wait()
    extended = ext[...]
    piece_rows = lax.broadcasted_iota(jnp.int32, (128, 1), 0)
    is_own = (piece_rows >= 2 * position) & (piece_rows < 2 * position + 2)
    own_mask = jnp.where(is_own, 1.0, 0.0)

    for first, size in PIECES:
        rows = pl.ds(first, size)
        if first == FINE:
            for copy in coarse:
                copy.wait()
            table = coarse_tiles[...].reshape(DEVICES * 32, 128)
            picked = jnp.concatenate([
                dot(column_hot(index_ref[:, 2048:2176] + part, 0, DEVICES * 32), table)
                for part in range(4)
            ], axis=1)
            blank = jnp.zeros((96, 512), f32)

            def placed(part):
                return jnp.concatenate([part, blank], axis=0)

            latents = placed(picked[0:32])
            joined[:, 0:512] = latents.astype(bf16)
            joined[:, 512:1024] = placed(picked[32:64]).astype(bf16)
            joined[:, 1024:1536] = placed(picked[64:96]).astype(bf16)
            masked[rows, :] = (latents * own_mask).astype(bf16)
            coarse_cot[...] = placed(picked[96:128])
            before = dot(joined[...], w1_ref[...]) + b1_row
        else:
            picker = column_hot(index_ref[:, first:first + size], 0, EXTENDED)
            before = before_ref[rows, :] + dot(
                dot(picker, extended).astype(bf16), w1_ref[512:1024, :]
            )
        before_ref[rows, :] = before
        hidden = (before * jax.nn.sigmoid(before)).astype(bf16)
        hidden_ref[rows, :] = hidden
        after = dot(hidden, w2_ref[...]) + b2_row
        normed, inv_scale = layer_norm_parts(after)
        normed_ref[rows, :] = normed
        own_latents = joined[:, 0:512] if first == FINE else edges_ref[rows, :]
        inv_ref[rows, :] = jnp.broadcast_to(inv_scale, (size, 128))
        updated_ref[rows, :] = (own_latents.astype(f32) + normed * gain).astype(bf16)
    coarse_rows = pl.ds(FINE, 128)
    hidden_ref[coarse_rows, :] = (hidden_ref[coarse_rows, :].astype(f32) * own_mask).astype(bf16)

    to_receiver = row_hot(index_ref[:, 896:1792], OWN)
    summed = dot(to_receiver, updated_ref[...])

    loads[3].wait()
    loads[4].wait()
    loads[5].wait()
    summed_low = summed.astype(bf16)
    node_before = dot(nodes, v1_ref[0:512, :]) + dot(summed_low, v1_ref[512:1024, :]) + c1_row
    sigma = jax.nn.sigmoid(node_before)
    node_hidden = (node_before * sigma).astype(bf16)
    node_normed, node_inv = layer_norm_parts(dot(node_hidden, v2_ref[...]) + c2_row)
    node_cot = node_cot_ref[...].astype(f32)
    node_after = gradient_after(node_cot, node_gain, node_normed, node_inv).astype(bf16)
    node_low = (
        contract_cols(node_after, v2_ref[...]) * sigma * (1.0 + node_before * (1.0 - sigma))
    ).astype(bf16)
    grad_summed = contract_cols(node_low, v1_ref[512:1024, :])
    for part in range(4):
        coarse_sums[position, part:part + 1, :] = grad_summed[0:1, 128 * part:128 * part + 128]
    sums = []
    for k in range(1, DEVICES):
        _, device = flat(k)
        sender, _ = flat(-k)
        remote(
            coarse_sums.at[position], coarse_sums.at[position],
            sums_send.at[k], sums_recv.at[k], device,
        ).start()
        sums.append(remote(
            coarse_sums.at[position], coarse_sums.at[sender],
            sums_send.at[k], sums_recv.at[k], device,
        ))

    grads, mine, passing, crossed = (g0, g1, g2, g3), (a0, a1, a2, a3), (b0, b1, b2, b3), (c0, c1, c2, c3)
    totals, along, arrived = (t0, t1, t2, t3), (d0, d1, d2, d3), (e0, e1, e2, e3)
    partner_core = (group, column * 2 + (1 - core), sub)
    partner_column = (group, (1 - column) * 2 + core, sub)

    def core_copy(n, which):
        return remote(
            grads[n].at[which * 2 + (1 - core)], mine[n].at[which],
            s1_send.at[n, which], s1_recv.at[n, which], partner_core,
        )

    def start_core(n):
        core_copy(n, 1 - column).start()
        core_copy(n, column).start()

    def column_copy(n):
        return remote(passing[n], crossed[n], s2_send.at[n], s2_recv.at[n], partner_column)

    def start_column(n):
        core_copy(n, 1 - column).wait()
        passing[n][...] = (
            grads[n][(1 - column) * 2 + core].astype(f32) + mine[n][1 - column].astype(f32)
        ).astype(bf16)
        column_copy(n).start()

    def total_column(n):
        core_copy(n, column).wait()
        column_copy(n).wait()
        totals[n][...] = (
            grads[n][column * 2 + core].astype(f32)
            + mine[n][column].astype(f32)
            + crossed[n][...].astype(f32)
        )

    def line_copy(n, way, block):
        step = 1 if way == 0 else SIDE - 1
        return remote(
            along[n].at[way, block], arrived[n].at[way, block],
            s3_send.at[n, way, block], s3_recv.at[n, way, block],
            (group, region, lax.rem(sub + step, SIDE)),
        )

    def pass_on(n, way, block):
        line_copy(n, way, block).wait_recv()
        along[n][way, block] = (
            totals[n][block] + arrived[n][way, block].astype(f32)
        ).astype(bf16)
        line_copy(n, way, block).start()

    def line_begin(n):
        for way, first in ((0, 0), (1, SIDE - 1)):
            @pl.when(sub == first)
            def _():
                for k in range(SIDE - 1):
                    block = 3 - k if way == 0 else k
                    along[n][way, block] = totals[n][block].astype(bf16)
                    line_copy(n, way, block).start()

    def line_step(n, k):
        for here, moves in (
            (1, (((0, 3),), ((0, 2), (1, 0)))), (2, (((1, 0),), ((1, 1), (0, 3))))
        ):
            @pl.when(sub == here)
            def _():
                for way, block in moves[k]:
                    pass_on(n, way, block)

    def line_end(n):
        @pl.when(sub > 0)
        def _():
            line_copy(n, 0, sub).wait_recv()
            totals[n][sub] = totals[n][sub] + arrived[n][0, sub].astype(f32)

        @pl.when(sub < SIDE - 1)
        def _():
            line_copy(n, 1, sub).wait_recv()
            totals[n][sub] = totals[n][sub] + arrived[n][1, sub].astype(f32)

        for k in range(SIDE - 1):
            @pl.when(sub < 3 - k)
            def _():
                line_copy(n, 0, 3 - k).wait_send()

            @pl.when(sub > k)
            def _():
                line_copy(n, 1, k).wait_send()
        return totals[n][sub]

    node_inner_grad = jnp.concatenate(
        [contract_rows(nodes, node_low), contract_rows(summed_low, node_low)], axis=0
    ).astype(bf16)
    node_outer_grad = contract_rows(node_hidden, node_after).astype(bf16)
    g0[:, :, 0:64, :] = node_inner_grad.reshape(SIDE, SIDE, 64, 512)
    g0[:, :, 64:96, :] = node_outer_grad.reshape(SIDE, SIDE, 32, 512)
    start_core(0)
    node_direct = node_cot + contract_cols(node_low, v1_ref[0:512, :])

    sums_high, sums_low = two_parts(grad_summed)
    for first, size in PIECES:
        rows = pl.ds(first, size)
        if first == FINE:
            for copy in sums:
                copy.wait()
            gathered = jnp.concatenate([coarse_sums[:, part, :] for part in range(4)], axis=1)
            gathered = jnp.concatenate([gathered, jnp.zeros((OWN - DEVICES, 512), f32)], axis=0)
            high, low = two_parts(gathered)
            picker = column_hot(index_ref[:, 2176:2304], 0, OWN)
            total = coarse_cot[...] + (dot(picker, high) + dot(picker, low))
        else:
            picker = column_hot(index_ref[:, 896 + first:896 + first + size], 0, OWN)
            total = edge_cot_ref[rows, :].astype(f32) + (dot(picker, sums_high) + dot(picker, sums_low))
        after_low = gradient_after(
            total, gain, normed_ref[rows, :], inv_ref[rows, 0:1]
        ).astype(bf16)
        after_low_ref[rows, :] = after_low
        before = before_ref[rows, :]
        sigma = jax.nn.sigmoid(before)
        before_low = (
            contract_cols(after_low, w2_ref[...]) * sigma * (1.0 + before * (1.0 - sigma))
        ).astype(bf16)
        before_low_ref[rows, :] = before_low
        direct = total + contract_cols(before_low, w1_ref[0:512, :])
        if first == FINE:
            row_pair = [
                jnp.sum(jnp.where(piece_rows == 2 * position + j, direct, 0.0), axis=0, keepdims=True)
                for j in range(2)
            ]
            is_second = lax.broadcasted_iota(jnp.int32, (2, 512), 0) == 1
            grad_coarse_ref[...] = jnp.where(is_second, row_pair[1], row_pair[0]).astype(bf16)
        else:
            grad_edges_ref[rows, :] = direct.astype(bf16)
        if first == 256:
            start_column(0)

    g1[...] = contract_rows(hidden_ref[...], after_low_ref[...]).astype(bf16).reshape(g1.shape)
    start_core(1)
    to_sender = row_hot(index_ref[:, 0:896], EXTENDED)
    from_high, from_low = two_parts(dot(to_sender, before_low_ref[...]))
    to_high, to_low = two_parts(dot(to_receiver, before_low_ref[...]))
    w1b, w1c = w1_ref[512:1024, :], w1_ref[1024:1536, :]
    from_grads = contract_cols(from_high, w1b) + contract_cols(from_low, w1b)
    send_back[...] = from_grads[OWN:].astype(bf16)
    back = []
    for m, (dr, ds) in enumerate(OFFSETS):
        slot = pl.ds(m * SLOT, SLOT)
        copy = remote(
            send_back.at[slot], returned.at[slot],
            back_send.at[m], back_recv.at[m], at(region - dr, sub - ds),
        )
        copy.start()
        back.append(copy)
    for n, buffer in ((2, g2), (3, g3)):
        cols = slice(256 * (n - 2), 256 * (n - 2) + 256)
        inner = jnp.concatenate([
            contract_rows(masked[...], before_low_ref[:, cols]),
            contract_rows(extended, from_high[:, cols]) + contract_rows(extended, from_low[:, cols]),
            contract_rows(nodes, to_high[:, cols]) + contract_rows(nodes, to_low[:, cols]),
        ], axis=0)
        buffer[...] = inner.astype(bf16).reshape(buffer.shape)
        start_core(n)
        if n == 2:
            start_column(1)
    start_column(2)
    total_column(0)
    line_begin(0)
    own = node_direct + from_grads[0:OWN]
    own = own + (contract_cols(to_high, w1c) + contract_cols(to_low, w1c))
    start_column(3)
    line_step(0, 0)
    total_column(1)
    line_begin(1)
    line_step(0, 1)
    for copy in back:
        copy.wait()
    own = own + dot(row_hot(send_row, OWN), returned[...])
    grad_nodes_ref[...] = own.astype(bf16)
    line_step(1, 0)
    total_column(2)
    line_begin(2)
    line_step(1, 1)
    node_block = line_end(0)
    out_ni_ref[...] = node_block[0:64]
    out_no_ref[...] = node_block[64:96]
    line_step(2, 0)
    total_column(3)
    line_begin(3)
    line_step(2, 1)
    out_eo_ref[...] = line_end(1)
    line_step(3, 0)
    line_step(3, 1)
    out_ei_ref[:, 0:256] = line_end(2)
    out_ei_ref[:, 256:512] = line_end(3)


def hand_over(*refs):
    held, sems = refs[14:21], refs[21]
    inward = [pltpu.make_async_copy(refs[n], held[n], sems.at[0, n]) for n in range(7)]
    outward = [pltpu.make_async_copy(held[n], refs[7 + n], sems.at[1, n]) for n in range(7)]
    for copy in inward:
        copy.start()
    for n in range(7):
        inward[n].wait()
        outward[n].start()
    for copy in outward:
        copy.wait()


def fused_device(
    node_latents, edge_latents, coarse_latents, node_cotangent, edge_cotangent, coarse_cotangent,
    edge_inner, edge_inner_bias, edge_outer, edge_outer_bias, edge_gain,
    node_inner, node_inner_bias, node_outer, node_outer_bias, node_gain,
    send_list, edge_sender, edge_receiver, coarse_sender, coarse_receiver,
):
    bf16, f32, dma = jnp.bfloat16, jnp.float32, pltpu.SemaphoreType.DMA
    position = lax.axis_index("region") * SIDE + lax.axis_index("sub")
    halo_slot = jnp.maximum(edge_sender - OWN, 0) // send_list.shape[2]
    padded_sender = edge_sender + halo_slot * (SLOT - send_list.shape[2])
    none = jnp.full((96,), -1, jnp.int32)
    every = jnp.arange(2 * DEVICES, dtype=jnp.int32)
    tile_row = 32 * (every // 2) + 4 * (every % 2)
    index = jnp.concatenate([
        padded_sender, jnp.where(coarse_sender == position, 0, -1), none,
        edge_receiver, jnp.where(coarse_receiver == position, 0, -1), none,
        jnp.pad(send_list[0], ((0, 0), (0, SLOT - send_list.shape[2])), constant_values=-1).reshape(-1),
        tile_row + 4, 32 * coarse_sender, 32 * coarse_receiver, tile_row + 12,
        coarse_receiver, none,
    ]).reshape(1, -1)
    blank = jnp.zeros((512,), f32)
    params = jnp.stack([
        edge_inner_bias, edge_outer_bias, edge_gain,
        node_inner_bias, node_outer_bias, node_gain, blank, blank,
    ])
    packet = jnp.concatenate(
        [node_latents[:1], coarse_latents, coarse_cotangent, jnp.zeros((3, 512), bf16)], axis=0
    ).reshape(32, 128)

    def per_chunk(make):
        return [pltpu.VMEM(*make(rows, cols)) for rows, cols in CHUNKS]

    scratch = [
        pltpu.VMEM((FINE, 512), bf16),
        pltpu.VMEM((FINE, 512), bf16),
        pltpu.VMEM((1536, 512), bf16),
        pltpu.VMEM((512, 512), bf16),
        pltpu.VMEM((1024, 512), bf16),
        pltpu.VMEM((512, 512), bf16),
        dma((6,)),
        pltpu.VMEM((128, 1536), bf16),
        pltpu.VMEM((EXTENDED, 512), bf16),
        pltpu.VMEM((8 * SLOT, 512), bf16),
        pltpu.VMEM((DEVICES, 32, 128), bf16),
        pltpu.VMEM((ROWS, 512), f32),
        pltpu.VMEM((ROWS, 512), bf16),
        pltpu.VMEM((ROWS, 512), f32),
        pltpu.VMEM((ROWS, 128), f32),
        pltpu.VMEM((ROWS, 512), bf16),
        pltpu.VMEM((ROWS, 512), bf16),
        pltpu.VMEM((ROWS, 512), bf16),
        pltpu.VMEM((ROWS, 512), bf16),
        pltpu.VMEM((8 * SLOT, 512), bf16),
        pltpu.VMEM((8 * SLOT, 512), bf16),
        pltpu.VMEM((128, 512), f32),
        pltpu.VMEM((DEVICES, 4, 128), f32),
        *per_chunk(lambda n, c: ((SIDE, SIDE, n, c), bf16)),
        *per_chunk(lambda n, c: ((2, SIDE, n, c), bf16)),
        *per_chunk(lambda n, c: ((SIDE, n, c), bf16)),
        *per_chunk(lambda n, c: ((SIDE, n, c), bf16)),
        *per_chunk(lambda n, c: ((SIDE, n, c), f32)),
        *per_chunk(lambda n, c: ((2, SIDE, n, c), bf16)),
        *per_chunk(lambda n, c: ((2, SIDE, n, c), bf16)),
        dma((8,)), dma((8,)), dma((DEVICES,)), dma((DEVICES,)), dma((DEVICES,)), dma((DEVICES,)),
        dma((8,)), dma((8,)), dma((4, 2)), dma((4, 2)), dma((4,)), dma((4,)),
        dma((4, 2, SIDE)), dma((4, 2, SIDE)),
    ]
    shape = jax.ShapeDtypeStruct
    vmem = pl.BlockSpec(memory_space=pltpu.VMEM)
    hbm = pl.BlockSpec(memory_space=pl.ANY)
    results = pl.pallas_call(
        step_kernel,
        out_shape=(
            shape((OWN, 512), bf16), shape((FINE, 512), bf16), shape((2, 512), bf16),
            shape((96, 512), f32), shape((32, 512), f32), shape((64, 512), f32), shape((32, 512), f32),
        ),
        in_specs=[vmem] * 4 + [hbm, vmem] + [hbm] * 5,
        out_specs=(vmem,) * 7,
        scratch_shapes=scratch,
        compiler_params=pltpu.CompilerParams(
            collective_id=0, has_side_effects=True, vmem_limit_bytes=58 * 2**20
        ),
    )(
        index, params, packet, node_latents, edge_latents, node_cotangent, edge_cotangent,
        edge_inner, edge_outer, node_inner, node_outer,
    )
    return pl.pallas_call(
        hand_over,
        out_shape=tuple(shape(result.shape, result.dtype) for result in results),
        in_specs=[hbm] * 7,
        out_specs=(hbm,) * 7,
        scratch_shapes=[pltpu.VMEM(result.shape, result.dtype) for result in results] + [dma((2, 7))],
    )(*results)


def solution(mesh):
    in_specs = (
        P(("groups", "region", "sub"), None),
        P(("groups", "region", "sub"), None),
        P(("groups", "region", "sub"), None),
        P(("groups", "region", "sub"), None),
        P(("groups", "region", "sub"), None),
        P(("groups", "region", "sub"), None),
        P(),
        P(),
        P(),
        P(),
        P(),
        P(),
        P(),
        P(),
        P(),
        P(),
        P(("groups", "region", "sub"), None, None),
        P(("groups", "region", "sub")),
        P(("groups", "region", "sub")),
        P("groups"),
        P("groups"),
    )
    out_specs = (
        P(("groups", "region", "sub"), None),
        P(("groups", "region", "sub"), None),
        P(("groups", "region", "sub"), None),
        P(("groups", "region", "sub"), None),
        P(("groups", "region", "sub"), None),
        P(("groups", "region", "sub"), None),
        P(("groups", "region", "sub"), None),
    )
    small = mesh.shape["region"] == SIDE and mesh.shape["sub"] == SIDE
    return jax.shard_map(
        fused_device if small else per_device, mesh=mesh, in_specs=in_specs, out_specs=out_specs, check_vma=False
    )
```

```python
import jax
import jax.numpy as jnp
from jax import lax
from jax.experimental import pallas as pl
from jax.experimental.pallas import tpu as pltpu
from jax.sharding import PartitionSpec as P


def passed_along(value, axis, steps):
    count = lax.axis_size(axis)
    pairs = [(source, (source + steps) % count) for source in range(count)]
    return lax.ppermute(value, axis, pairs)


def for_sending(array):

    def short(part):
        return part.astype(jnp.bfloat16) if part.dtype == jnp.float32 else part

    return jax.tree.map(short, array)


def network_forward(inputs, inner, inner_bias, outer, outer_bias, gain):
    before = jnp.dot(inputs, inner, preferred_element_type=jnp.float32) + inner_bias
    hidden = jax.nn.silu(before).astype(jnp.bfloat16)
    after = jnp.dot(hidden, outer, preferred_element_type=jnp.float32) + outer_bias
    centred = after - jnp.mean(after, axis=-1, keepdims=True)
    inv_scale = lax.rsqrt(jnp.mean(centred * centred, axis=-1, keepdims=True) + 1e-05)
    normed = centred * inv_scale
    return (normed * gain, (before, hidden, normed, inv_scale))


def contract_rows(left, right):
    return lax.dot_general(
        left, right, (((0,), (0,)), ((), ())), preferred_element_type=jnp.float32
    )


def contract_cols(left, right):
    return lax.dot_general(
        left, right, (((1,), (1,)), ((), ())), preferred_element_type=jnp.float32
    )


def network_backward(upstream, inputs, inner, outer, gain, stored):
    before, hidden, normed, inv_scale = stored
    scaled = upstream * gain
    grad_after = inv_scale * (
        scaled
        - jnp.mean(scaled, axis=-1, keepdims=True)
        - normed * jnp.mean(scaled * normed, axis=-1, keepdims=True)
    )
    after_low = grad_after.astype(jnp.bfloat16)
    outer_grad = contract_rows(hidden, after_low)
    sigma = jax.nn.sigmoid(before)
    grad_before = contract_cols(after_low, outer) * sigma * (1.0 + before * (1.0 - sigma))
    before_low = grad_before.astype(jnp.bfloat16)
    inner_grad = contract_rows(inputs, before_low)
    input_grad = contract_cols(before_low, inner)
    return (input_grad, inner_grad, outer_grad)


def onehot_sum(targets, count, values):
    picker = (targets[None, :] == jnp.arange(count, dtype=jnp.int32)[:, None]).astype(jnp.float32)
    return jnp.dot(
        picker, values, preferred_element_type=jnp.float32, precision=lax.Precision.HIGHEST
    )


def with_centre(blocks):
    empty = jnp.zeros((1,) + blocks.shape[1:], blocks.dtype)
    grid = jnp.concatenate([blocks[:4], empty, blocks[4:]], axis=0)
    return grid.reshape((3, 3) + blocks.shape[1:])


def without_centre(grid):
    flat = grid.reshape((9,) + grid.shape[2:])
    return jnp.concatenate([flat[:4], flat[5:]], axis=0)


def per_device(
    node_latents,
    edge_latents,
    coarse_latents,
    node_cotangent,
    edge_cotangent,
    coarse_cotangent,
    edge_inner,
    edge_inner_bias,
    edge_outer,
    edge_outer_bias,
    edge_gain,
    node_inner,
    node_inner_bias,
    node_outer,
    node_outer_bias,
    node_gain,
    send_list,
    edge_sender,
    edge_receiver,
    coarse_sender,
    coarse_receiver,
):
    latent = node_latents.shape[1]
    local_rows = node_latents.shape[0]
    region_count = lax.axis_size("region")
    sub_count = lax.axis_size("sub")
    device_count = region_count * sub_count
    position = lax.axis_index(("region", "sub"))
    neighbours = send_list.shape[1]
    halo_rows = send_list.shape[2]
    send_rows = send_list[0].reshape(-1)
    outgoing = node_latents[send_rows].reshape(neighbours, halo_rows, latent)
    grid = with_centre(outgoing)
    region_moved = [passed_along(grid[step + 1], "region", step) for step in (-1, 1)]
    sectioned = jnp.stack([region_moved[0], grid[1], region_moved[1]], axis=0)
    sub_moved = [passed_along(sectioned[:, step + 1], "sub", step) for step in (-1, 1)]
    incoming = without_centre(jnp.stack([sub_moved[0], sectioned[:, 1], sub_moved[1]], axis=1))
    extended = jnp.concatenate(
        [node_latents, incoming.reshape(neighbours * halo_rows, latent)], axis=0
    )
    inputs = jnp.concatenate(
        [edge_latents, extended[edge_sender], node_latents[edge_receiver]], axis=1
    )
    message, edge_stored = network_forward(
        inputs, edge_inner, edge_inner_bias, edge_outer, edge_outer_bias, edge_gain
    )
    updated = (edge_latents.astype(jnp.float32) + message).astype(jnp.bfloat16)
    receive_low = (
        edge_receiver[None, :] == jnp.arange(local_rows, dtype=jnp.int32)[:, None]
    ).astype(jnp.bfloat16)
    summed = jnp.dot(receive_low, updated, preferred_element_type=jnp.float32)
    coarse_rows = 1
    coarse_edges = coarse_latents.shape[0]
    own_nodes = node_latents[:coarse_rows]
    coarse_nodes, coarse_edge_rows, coarse_upstream = (
        lax.all_gather(own_nodes, ("region", "sub"), axis=0, tiled=True),
        lax.all_gather(coarse_latents, ("region", "sub"), axis=0, tiled=True),
        lax.all_gather(coarse_cotangent, ("region", "sub"), axis=0, tiled=True),
    )
    coarse_inputs = jnp.concatenate(
        [coarse_edge_rows, coarse_nodes[coarse_sender], coarse_nodes[coarse_receiver]], axis=1
    )
    coarse_message, coarse_stored = network_forward(
        coarse_inputs, edge_inner, edge_inner_bias, edge_outer, edge_outer_bias, edge_gain
    )
    coarse_updated = (coarse_edge_rows.astype(jnp.float32) + coarse_message).astype(jnp.bfloat16)
    coarse_summed = jax.ops.segment_sum(
        coarse_updated.astype(jnp.float32), coarse_receiver, num_segments=device_count
    )
    coarse_own = lax.dynamic_slice_in_dim(coarse_summed, position * coarse_rows, coarse_rows)
    summed = summed.at[:coarse_rows].add(coarse_own)
    node_inputs = jnp.concatenate([node_latents, summed.astype(jnp.bfloat16)], axis=1)
    unused_out, node_stored = network_forward(
        node_inputs, node_inner, node_inner_bias, node_outer, node_outer_bias, node_gain
    )
    node_grad, node_inner_grad, node_outer_grad = network_backward(
        node_cotangent.astype(jnp.float32),
        node_inputs,
        node_inner,
        node_outer,
        node_gain,
        node_stored,
    )
    grad_nodes = node_cotangent.astype(jnp.float32) + node_grad[:, :latent]
    grad_summed = node_grad[:, latent:]
    total = edge_cotangent.astype(jnp.float32) + grad_summed[edge_receiver]
    edge_grad, fine_inner, fine_outer = network_backward(
        total, inputs, edge_inner, edge_outer, edge_gain, edge_stored
    )
    grad_edges = (total + edge_grad[:, :latent]).astype(jnp.bfloat16)
    extended_grads = onehot_sum(
        edge_sender, local_rows + neighbours * halo_rows, edge_grad[:, latent : 2 * latent]
    )
    grad_nodes = grad_nodes + extended_grads[:local_rows]
    grad_nodes = grad_nodes + onehot_sum(edge_receiver, local_rows, edge_grad[:, 2 * latent :])
    returning = extended_grads[local_rows:].reshape(neighbours, halo_rows, latent)
    back_grid = with_centre(returning)
    sub_back = [
        passed_along(back_grid[:, step + 1].astype(jnp.bfloat16), "sub", -step).astype(jnp.float32)
        for step in (-1, 1)
    ]
    sectioned_back = jnp.stack([sub_back[0], back_grid[:, 1], sub_back[1]], axis=1)
    region_back = [
        passed_along(for_sending(sectioned_back[step + 1]), "region", -step) for step in (-1, 1)
    ]
    returned = without_centre(
        jnp.stack([region_back[0], sectioned_back[1], region_back[1]], axis=0)
    )
    grad_nodes = grad_nodes + onehot_sum(
        send_rows, local_rows, returned.reshape(neighbours * halo_rows, latent)
    )
    coarse_needed = lax.all_gather(grad_summed[:coarse_rows], ("region", "sub"), axis=0, tiled=True)
    coarse_total = coarse_upstream.astype(jnp.float32) + coarse_needed[coarse_receiver]
    coarse_grad, coarse_inner, coarse_outer = network_backward(
        coarse_total, coarse_inputs, edge_inner, edge_outer, edge_gain, coarse_stored
    )
    coarse_edge_grads = (coarse_total + coarse_grad[:, :latent]).astype(jnp.bfloat16)
    coarse_node_grads = jax.ops.segment_sum(
        coarse_grad[:, latent : 2 * latent], coarse_sender, num_segments=device_count
    )
    coarse_node_grads = coarse_node_grads + jax.ops.segment_sum(
        coarse_grad[:, 2 * latent :], coarse_receiver, num_segments=device_count
    )
    grad_coarse = lax.dynamic_slice_in_dim(coarse_edge_grads, position * coarse_edges, coarse_edges)
    own_grads = lax.dynamic_slice_in_dim(coarse_node_grads, position * coarse_rows, coarse_rows)
    only_first = (position == 0).astype(jnp.float32)
    coarse_inner = coarse_inner * only_first
    coarse_outer = coarse_outer * only_first
    grad_nodes = grad_nodes.at[:coarse_rows].add(own_grads)
    weight_terms = (
        fine_inner + coarse_inner,
        fine_outer + coarse_outer,
        node_inner_grad,
        node_outer_grad,
    )
    reduced = (
        lax.psum_scatter(weight_terms[0], ("region", "sub"), scatter_dimension=0, tiled=True),
        lax.psum_scatter(weight_terms[1], ("region", "sub"), scatter_dimension=0, tiled=True),
        lax.psum_scatter(weight_terms[2], ("region", "sub"), scatter_dimension=0, tiled=True),
        lax.psum_scatter(weight_terms[3], ("region", "sub"), scatter_dimension=0, tiled=True),
    )
    return (
        grad_nodes.astype(jnp.bfloat16),
        grad_edges,
        grad_coarse,
        reduced[0],
        reduced[1],
        reduced[2],
        reduced[3],
    )


def dot(left, right):
    return jnp.dot(left, right, preferred_element_type=jnp.float32)


def one_hot(hits):
    return jnp.where(hits, 1.0, 0.0).astype(jnp.bfloat16)


def column_hot(row, first, count):
    tall = jnp.transpose(jnp.broadcast_to(row, (128, row.shape[1])))
    lanes = lax.broadcasted_iota(jnp.int32, tall.shape, 1)
    parts = [one_hot(tall == lanes + (first + at)) for at in range(0, count, 128)]
    return jnp.concatenate(parts, axis=1) if len(parts) > 1 else parts[0]


def row_hot(row, count):
    shape = (count, row.shape[1])
    rows = lax.broadcasted_iota(jnp.int32, shape, 0)
    return one_hot(jnp.broadcast_to(row, shape) == rows)


def two_parts(value):
    high = value.astype(jnp.bfloat16)
    return high, (value - high.astype(jnp.float32)).astype(jnp.bfloat16)


def layer_norm_parts(after):
    centred = after - jnp.mean(after, axis=-1, keepdims=True)
    inv_scale = lax.rsqrt(jnp.mean(centred * centred, axis=-1, keepdims=True) + 1e-05)
    return centred * inv_scale, inv_scale


def gradient_after(upstream, gain, normed, inv_scale):
    scaled = upstream * gain
    return inv_scale * (
        scaled
        - jnp.mean(scaled, axis=-1, keepdims=True)
        - normed * jnp.mean(scaled * normed, axis=-1, keepdims=True)
    )


OFFSETS = ((-1, -1), (-1, 0), (-1, 1), (0, -1), (0, 1), (1, -1), (1, 0), (1, 1))
SLOT = 32
SIDE = 4
DEVICES = SIDE * SIDE
FINE = 768
ROWS = 896
OWN = 128
EXTENDED = OWN + 8 * SLOT
PIECES = ((0, 256), (256, 256), (512, 256), (768, 128))
CHUNKS = ((96, 512), (32, 512), (96, 256), (96, 256))


def step_kernel(
    index_ref, p0, p1, p2, p3, p4, p5, coarse_lat_ref, coarse_cot_in, from_ref, into_ref,
    nodes_ref, edges_hbm, node_cot_ref, edge_cot_hbm, w1_hbm, w2_hbm, v1_hbm, v2_hbm,
    grad_nodes_ref, grad_edges_ref, grad_coarse_ref,
    out_ei_ref, out_eo_ref, out_ni_ref, out_no_ref,
    edges_ref, edge_cot_ref, w1_ref, w2_ref, v1_ref, v2_ref, load_sems,
    joined, ext, outgoing, coarse_tiles, before_ref, hidden_ref, normed_ref, inv_ref,
    updated_ref, after_low_ref, before_low_ref, masked, send_back, returned,
    coarse_cot, coarse_sums,
    g0, g1, g2, g3, a0, a1, a2, a3, b0, b1, b2, b3, c0, c1, c2, c3,
    t0, t1, t2, t3, d0, d1, d2, d3, e0, e1, e2, e3,
    halo_send, halo_recv, coarse_send, coarse_recv, sums_send, sums_recv,
    back_send, back_recv, s1_send, s1_recv, s2_send, s2_recv, s3_send, s3_recv,
):
    bf16, f32 = jnp.bfloat16, jnp.float32
    group = lax.axis_index("groups")
    region = lax.axis_index("region")
    sub = lax.axis_index("sub")
    position = region * SIDE + sub
    core = lax.rem(region, 2)
    column = lax.div(region, 2)

    def at(r, s):
        return (group, lax.rem(r + SIDE, SIDE), lax.rem(s + SIDE, SIDE))

    def flat(k):
        other = lax.rem(position + k + DEVICES, DEVICES)
        return other, (group, lax.div(other, SIDE), lax.rem(other, SIDE))

    def remote(src, dst, send, recv, device):
        return pltpu.make_async_remote_copy(
            src_ref=src, dst_ref=dst, send_sem=send, recv_sem=recv,
            device_id=device, device_id_type=pl.DeviceIdType.MESH,
        )

    loads = [
        pltpu.make_async_copy(src, dst, load_sems.at[n])
        for n, (src, dst) in enumerate((
            (edges_hbm, edges_ref), (w1_hbm, w1_ref), (w2_hbm, w2_ref),
            (v1_hbm, v1_ref), (v2_hbm, v2_ref), (edge_cot_hbm, edge_cot_ref),
        ))
    ]
    barrier = pltpu.get_barrier_semaphore()
    for k in range(1, DEVICES):
        pl.semaphore_signal(
            barrier, inc=1, device_id=flat(k)[1], device_id_type=pl.DeviceIdType.MESH
        )
    for load in loads:
        load.start()
    nodes = nodes_ref[...]
    send_row = index_ref[:, 256:512]
    outgoing[...] = dot(column_hot(send_row, 0, OWN), nodes).astype(bf16)
    tile_rows = lax.broadcasted_iota(jnp.int32, (32, 128), 0)
    tile = jnp.zeros((32, 128), f32)
    packed = (
        nodes_ref[0:16, :].astype(f32)[0:1],
        *(coarse_lat_ref[...].astype(f32)[j:j + 1] for j in range(2)),
        *(coarse_cot_in[...].astype(f32)[j:j + 1] for j in range(2)),
    )
    for n, row in enumerate(packed):
        for part in range(4):
            tile = jnp.where(tile_rows == 4 * n + part, row[:, 128 * part:128 * part + 128], tile)
    coarse_tiles[position] = tile.astype(bf16)
    ext[0:OWN, :] = nodes
    pl.semaphore_wait(barrier, DEVICES - 1)

    waits = []
    halo = []
    for m, (dr, ds) in enumerate(OFFSETS):
        slot = pl.ds(OWN + m * SLOT, SLOT)
        copy = remote(
            outgoing.at[pl.ds(m * SLOT, SLOT)], ext.at[slot],
            halo_send.at[m], halo_recv.at[m], at(region + dr, sub + ds),
        )
        copy.start()
        halo.append(copy)
    coarse = []
    for k in range(1, DEVICES):
        _, device = flat(k)
        sender, _ = flat(-k)
        remote(
            coarse_tiles.at[position], coarse_tiles.at[position],
            coarse_send.at[k], coarse_recv.at[k], device,
        ).start()
        coarse.append(remote(
            coarse_tiles.at[position], coarse_tiles.at[sender],
            coarse_send.at[k], coarse_recv.at[k], device,
        ))

    b1_row, b2_row, gain, c1_row, c2_row, node_gain = (
        vector[...].reshape(1, 512) for vector in (p0, p1, p2, p3, p4, p5)
    )
    from_row = from_ref[...].reshape(1, FINE)
    receiver = into_ref[...].reshape(1, FINE)
    slot_of = lax.shift_right_logical(jnp.maximum(from_row - OWN, 0) * 2731, 16)
    from_row = from_row + 8 * slot_of

    loads[0].wait()
    loads[1].wait()
    for first, size in PIECES[:3]:
        rows = pl.ds(first, size)
        masked[rows, :] = edges_ref[rows, :]
        picker = column_hot(receiver[:, first:first + size], 0, OWN)
        to_rows = dot(picker, nodes).astype(bf16)
        before_ref[rows, :] = (
            dot(edges_ref[rows, :], w1_ref[0:512, :]) + dot(to_rows, w1_ref[1024:1536, :]) + b1_row
        )
    loads[2].wait()
    for copy in halo:
        copy.wait()
    extended = ext[...]
    piece_rows = lax.broadcasted_iota(jnp.int32, (128, 1), 0)
    is_own = (piece_rows >= 2 * position) & (piece_rows < 2 * position + 2)
    own_mask = jnp.where(is_own, 1.0, 0.0)

    for first, size in PIECES:
        rows = pl.ds(first, size)
        if first == FINE:
            for copy in coarse:
                copy.wait()
            table = coarse_tiles[...].reshape(DEVICES * 32, 128)
            picked = jnp.concatenate([
                dot(column_hot(index_ref[:, 512:640] + part, 0, DEVICES * 32), table)
                for part in range(4)
            ], axis=1)
            blank = jnp.zeros((96, 512), f32)

            def placed(part):
                return jnp.concatenate([part, blank], axis=0)

            latents = placed(picked[0:32])
            joined[:, 0:512] = latents.astype(bf16)
            joined[:, 512:1024] = placed(picked[32:64]).astype(bf16)
            joined[:, 1024:1536] = placed(picked[64:96]).astype(bf16)
            masked[rows, :] = (latents * own_mask).astype(bf16)
            coarse_cot[...] = placed(picked[96:128])
            before = dot(joined[...], w1_ref[...]) + b1_row
        else:
            picker = column_hot(from_row[:, first:first + size], 0, EXTENDED)
            before = before_ref[rows, :] + dot(
                dot(picker, extended).astype(bf16), w1_ref[512:1024, :]
            )
        before_ref[rows, :] = before
        hidden = (before * jax.nn.sigmoid(before)).astype(bf16)
        hidden_ref[rows, :] = hidden
        after = dot(hidden, w2_ref[...]) + b2_row
        normed, inv_scale = layer_norm_parts(after)
        normed_ref[rows, :] = normed
        own_latents = joined[:, 0:512] if first == FINE else edges_ref[rows, :]
        inv_ref[rows, :] = jnp.broadcast_to(inv_scale, (size, 128))
        updated_ref[rows, :] = (own_latents.astype(f32) + normed * gain).astype(bf16)
    coarse_rows = pl.ds(FINE, 128)
    hidden_ref[coarse_rows, :] = (hidden_ref[coarse_rows, :].astype(f32) * own_mask).astype(bf16)

    to_receiver = row_hot(jnp.concatenate([receiver, index_ref[:, 128:256]], axis=1), OWN)
    summed = dot(to_receiver, updated_ref[...])

    loads[3].wait()
    loads[4].wait()
    loads[5].wait()
    summed_low = summed.astype(bf16)
    node_before = dot(nodes, v1_ref[0:512, :]) + dot(summed_low, v1_ref[512:1024, :]) + c1_row
    sigma = jax.nn.sigmoid(node_before)
    node_hidden = (node_before * sigma).astype(bf16)
    node_normed, node_inv = layer_norm_parts(dot(node_hidden, v2_ref[...]) + c2_row)
    node_cot = node_cot_ref[...].astype(f32)
    node_after = gradient_after(node_cot, node_gain, node_normed, node_inv).astype(bf16)
    node_low = (
        contract_cols(node_after, v2_ref[...]) * sigma * (1.0 + node_before * (1.0 - sigma))
    ).astype(bf16)
    grad_summed = contract_cols(node_low, v1_ref[512:1024, :])
    for part in range(4):
        coarse_sums[position, part:part + 1, :] = grad_summed[0:1, 128 * part:128 * part + 128]
    sums = []
    for k in range(1, DEVICES):
        _, device = flat(k)
        sender, _ = flat(-k)
        remote(
            coarse_sums.at[position], coarse_sums.at[position],
            sums_send.at[k], sums_recv.at[k], device,
        ).start()
        sums.append(remote(
            coarse_sums.at[position], coarse_sums.at[sender],
            sums_send.at[k], sums_recv.at[k], device,
        ))

    grads, mine, passing, crossed = (g0, g1, g2, g3), (a0, a1, a2, a3), (b0, b1, b2, b3), (c0, c1, c2, c3)
    totals, along, arrived = (t0, t1, t2, t3), (d0, d1, d2, d3), (e0, e1, e2, e3)
    partner_core = (group, column * 2 + (1 - core), sub)
    partner_column = (group, (1 - column) * 2 + core, sub)

    def core_copy(n, which):
        return remote(
            grads[n].at[which * 2 + (1 - core)], mine[n].at[which],
            s1_send.at[n, which], s1_recv.at[n, which], partner_core,
        )

    def start_core(n):
        core_copy(n, 1 - column).start()
        core_copy(n, column).start()

    def column_copy(n):
        return remote(passing[n], crossed[n], s2_send.at[n], s2_recv.at[n], partner_column)

    def start_column(n):
        core_copy(n, 1 - column).wait()
        passing[n][...] = (
            grads[n][(1 - column) * 2 + core].astype(f32) + mine[n][1 - column].astype(f32)
        ).astype(bf16)
        column_copy(n).start()

    def total_column(n):
        core_copy(n, column).wait()
        column_copy(n).wait()
        totals[n][...] = (
            grads[n][column * 2 + core].astype(f32)
            + mine[n][column].astype(f32)
            + crossed[n][...].astype(f32)
        )

    def line_copy(n, way, block):
        step = 1 if way == 0 else SIDE - 1
        return remote(
            along[n].at[way, block], arrived[n].at[way, block],
            s3_send.at[n, way, block], s3_recv.at[n, way, block],
            (group, region, lax.rem(sub + step, SIDE)),
        )

    def pass_on(n, way, block):
        line_copy(n, way, block).wait_recv()
        along[n][way, block] = (
            totals[n][block] + arrived[n][way, block].astype(f32)
        ).astype(bf16)
        line_copy(n, way, block).start()

    def line_begin(n):
        for way, first in ((0, 0), (1, SIDE - 1)):
            @pl.when(sub == first)
            def _():
                for k in range(SIDE - 1):
                    block = 3 - k if way == 0 else k
                    along[n][way, block] = totals[n][block].astype(bf16)
                    line_copy(n, way, block).start()

    def line_step(n, k):
        for here, moves in (
            (1, (((0, 3),), ((0, 2), (1, 0)))), (2, (((1, 0),), ((1, 1), (0, 3))))
        ):
            @pl.when(sub == here)
            def _():
                for way, block in moves[k]:
                    pass_on(n, way, block)

    def line_end(n):
        @pl.when(sub > 0)
        def _():
            line_copy(n, 0, sub).wait_recv()
            totals[n][sub] = totals[n][sub] + arrived[n][0, sub].astype(f32)

        @pl.when(sub < SIDE - 1)
        def _():
            line_copy(n, 1, sub).wait_recv()
            totals[n][sub] = totals[n][sub] + arrived[n][1, sub].astype(f32)

        for k in range(SIDE - 1):
            @pl.when(sub < 3 - k)
            def _():
                line_copy(n, 0, 3 - k).wait_send()

            @pl.when(sub > k)
            def _():
                line_copy(n, 1, k).wait_send()
        return totals[n][sub]

    node_inner_grad = jnp.concatenate(
        [contract_rows(nodes, node_low), contract_rows(summed_low, node_low)], axis=0
    ).astype(bf16)
    node_outer_grad = contract_rows(node_hidden, node_after).astype(bf16)
    g0[:, :, 0:64, :] = node_inner_grad.reshape(SIDE, SIDE, 64, 512)
    g0[:, :, 64:96, :] = node_outer_grad.reshape(SIDE, SIDE, 32, 512)
    start_core(0)
    node_direct = node_cot + contract_cols(node_low, v1_ref[0:512, :])

    sums_high, sums_low = two_parts(grad_summed)
    for first, size in PIECES:
        rows = pl.ds(first, size)
        if first == FINE:
            for copy in sums:
                copy.wait()
            gathered = jnp.concatenate([coarse_sums[:, part, :] for part in range(4)], axis=1)
            gathered = jnp.concatenate([gathered, jnp.zeros((OWN - DEVICES, 512), f32)], axis=0)
            high, low = two_parts(gathered)
            picker = column_hot(index_ref[:, 640:768], 0, OWN)
            total = coarse_cot[...] + (dot(picker, high) + dot(picker, low))
        else:
            picker = column_hot(receiver[:, first:first + size], 0, OWN)
            total = edge_cot_ref[rows, :].astype(f32) + (dot(picker, sums_high) + dot(picker, sums_low))
        after_low = gradient_after(
            total, gain, normed_ref[rows, :], inv_ref[rows, 0:1]
        ).astype(bf16)
        after_low_ref[rows, :] = after_low
        before = before_ref[rows, :]
        sigma = jax.nn.sigmoid(before)
        before_low = (
            contract_cols(after_low, w2_ref[...]) * sigma * (1.0 + before * (1.0 - sigma))
        ).astype(bf16)
        before_low_ref[rows, :] = before_low
        direct = total + contract_cols(before_low, w1_ref[0:512, :])
        if first == FINE:
            row_pair = [
                jnp.sum(jnp.where(piece_rows == 2 * position + j, direct, 0.0), axis=0, keepdims=True)
                for j in range(2)
            ]
            is_second = lax.broadcasted_iota(jnp.int32, (2, 512), 0) == 1
            grad_coarse_ref[...] = jnp.where(is_second, row_pair[1], row_pair[0]).astype(bf16)
        else:
            grad_edges_ref[rows, :] = direct.astype(bf16)
        if first == 256:
            start_column(0)

    g1[...] = contract_rows(hidden_ref[...], after_low_ref[...]).astype(bf16).reshape(g1.shape)
    start_core(1)
    to_sender = row_hot(jnp.concatenate([from_row, index_ref[:, 0:128]], axis=1), EXTENDED)
    from_high, from_low = two_parts(dot(to_sender, before_low_ref[...]))
    to_high, to_low = two_parts(dot(to_receiver, before_low_ref[...]))
    w1b, w1c = w1_ref[512:1024, :], w1_ref[1024:1536, :]
    from_grads = contract_cols(from_high, w1b) + contract_cols(from_low, w1b)
    send_back[...] = from_grads[OWN:].astype(bf16)
    back = []
    for m, (dr, ds) in enumerate(OFFSETS):
        slot = pl.ds(m * SLOT, SLOT)
        copy = remote(
            send_back.at[slot], returned.at[slot],
            back_send.at[m], back_recv.at[m], at(region - dr, sub - ds),
        )
        copy.start()
        back.append(copy)
    for n, buffer in ((2, g2), (3, g3)):
        cols = slice(256 * (n - 2), 256 * (n - 2) + 256)
        inner = jnp.concatenate([
            contract_rows(masked[...], before_low_ref[:, cols]),
            contract_rows(extended, from_high[:, cols]) + contract_rows(extended, from_low[:, cols]),
            contract_rows(nodes, to_high[:, cols]) + contract_rows(nodes, to_low[:, cols]),
        ], axis=0)
        buffer[...] = inner.astype(bf16).reshape(buffer.shape)
        start_core(n)
        if n == 2:
            start_column(1)
    start_column(2)
    total_column(0)
    line_begin(0)
    own = node_direct + from_grads[0:OWN]
    own = own + (contract_cols(to_high, w1c) + contract_cols(to_low, w1c))
    start_column(3)
    line_step(0, 0)
    total_column(1)
    line_begin(1)
    line_step(0, 1)
    for copy in back:
        copy.wait()
    own = own + dot(row_hot(send_row, OWN), returned[...])
    grad_nodes_ref[...] = own.astype(bf16)
    line_step(1, 0)
    total_column(2)
    line_begin(2)
    line_step(1, 1)
    node_block = line_end(0)
    out_ni_ref[...] = node_block[0:64]
    out_no_ref[...] = node_block[64:96]
    line_step(2, 0)
    total_column(3)
    line_begin(3)
    line_step(2, 1)
    out_eo_ref[...] = line_end(1)
    line_step(3, 0)
    line_step(3, 1)
    out_ei_ref[:, 0:256] = line_end(2)
    out_ei_ref[:, 256:512] = line_end(3)


def hand_over(*refs):
    held, sems = refs[14:21], refs[21]
    inward = [pltpu.make_async_copy(refs[n], held[n], sems.at[0, n]) for n in range(7)]
    outward = [pltpu.make_async_copy(held[n], refs[7 + n], sems.at[1, n]) for n in range(7)]
    for copy in inward:
        copy.start()
    for n in range(7):
        inward[n].wait()
        outward[n].start()
    for copy in outward:
        copy.wait()


def fused_device(
    node_latents, edge_latents, coarse_latents, node_cotangent, edge_cotangent, coarse_cotangent,
    edge_inner, edge_inner_bias, edge_outer, edge_outer_bias, edge_gain,
    node_inner, node_inner_bias, node_outer, node_outer_bias, node_gain,
    send_list, edge_sender, edge_receiver, coarse_sender, coarse_receiver,
):
    bf16, f32, dma = jnp.bfloat16, jnp.float32, pltpu.SemaphoreType.DMA
    position = lax.axis_index("region") * SIDE + lax.axis_index("sub")
    none = jnp.full((96,), -1, jnp.int32)
    every = jnp.arange(2 * DEVICES, dtype=jnp.int32)
    tile_row = 32 * (every // 2) + 4 * (every % 2)
    index = jnp.concatenate([
        jnp.where(coarse_sender == position, 0, -1), none,
        jnp.where(coarse_receiver == position, 0, -1), none,
        jnp.pad(send_list[0], ((0, 0), (0, SLOT - send_list.shape[2])), constant_values=-1).reshape(-1),
        tile_row + 4, 32 * coarse_sender, 32 * coarse_receiver, tile_row + 12,
        coarse_receiver, none,
    ]).reshape(1, -1)
    def per_chunk(make):
        return [pltpu.VMEM(*make(rows, cols)) for rows, cols in CHUNKS]

    scratch = [
        pltpu.VMEM((FINE, 512), bf16),
        pltpu.VMEM((FINE, 512), bf16),
        pltpu.VMEM((1536, 512), bf16),
        pltpu.VMEM((512, 512), bf16),
        pltpu.VMEM((1024, 512), bf16),
        pltpu.VMEM((512, 512), bf16),
        dma((6,)),
        pltpu.VMEM((128, 1536), bf16),
        pltpu.VMEM((EXTENDED, 512), bf16),
        pltpu.VMEM((8 * SLOT, 512), bf16),
        pltpu.VMEM((DEVICES, 32, 128), bf16),
        pltpu.VMEM((ROWS, 512), f32),
        pltpu.VMEM((ROWS, 512), bf16),
        pltpu.VMEM((ROWS, 512), f32),
        pltpu.VMEM((ROWS, 128), f32),
        pltpu.VMEM((ROWS, 512), bf16),
        pltpu.VMEM((ROWS, 512), bf16),
        pltpu.VMEM((ROWS, 512), bf16),
        pltpu.VMEM((ROWS, 512), bf16),
        pltpu.VMEM((8 * SLOT, 512), bf16),
        pltpu.VMEM((8 * SLOT, 512), bf16),
        pltpu.VMEM((128, 512), f32),
        pltpu.VMEM((DEVICES, 4, 128), f32),
        *per_chunk(lambda n, c: ((SIDE, SIDE, n, c), bf16)),
        *per_chunk(lambda n, c: ((2, SIDE, n, c), bf16)),
        *per_chunk(lambda n, c: ((SIDE, n, c), bf16)),
        *per_chunk(lambda n, c: ((SIDE, n, c), bf16)),
        *per_chunk(lambda n, c: ((SIDE, n, c), f32)),
        *per_chunk(lambda n, c: ((2, SIDE, n, c), bf16)),
        *per_chunk(lambda n, c: ((2, SIDE, n, c), bf16)),
        dma((8,)), dma((8,)), dma((DEVICES,)), dma((DEVICES,)), dma((DEVICES,)), dma((DEVICES,)),
        dma((8,)), dma((8,)), dma((4, 2)), dma((4, 2)), dma((4,)), dma((4,)),
        dma((4, 2, SIDE)), dma((4, 2, SIDE)),
    ]
    shape = jax.ShapeDtypeStruct
    vmem = pl.BlockSpec(memory_space=pltpu.VMEM)
    hbm = pl.BlockSpec(memory_space=pl.ANY)
    results = pl.pallas_call(
        step_kernel,
        out_shape=(
            shape((OWN, 512), bf16), shape((FINE, 512), bf16), shape((2, 512), bf16),
            shape((96, 512), f32), shape((32, 512), f32), shape((64, 512), f32), shape((32, 512), f32),
        ),
        in_specs=[vmem] * 12 + [hbm, vmem] + [hbm] * 5,
        out_specs=(vmem,) * 7,
        scratch_shapes=scratch,
        compiler_params=pltpu.CompilerParams(
            collective_id=0, has_side_effects=True, vmem_limit_bytes=58 * 2**20
        ),
    )(
        index, edge_inner_bias, edge_outer_bias, edge_gain,
        node_inner_bias, node_outer_bias, node_gain, coarse_latents, coarse_cotangent,
        edge_sender, edge_receiver, node_latents, edge_latents, node_cotangent, edge_cotangent,
        edge_inner, edge_outer, node_inner, node_outer,
    )
    return pl.pallas_call(
        hand_over,
        out_shape=tuple(shape(result.shape, result.dtype) for result in results),
        in_specs=[hbm] * 7,
        out_specs=(hbm,) * 7,
        scratch_shapes=[pltpu.VMEM(result.shape, result.dtype) for result in results] + [dma((2, 7))],
    )(*results)


def solution(mesh):
    in_specs = (
        P(("groups", "region", "sub"), None),
        P(("groups", "region", "sub"), None),
        P(("groups", "region", "sub"), None),
        P(("groups", "region", "sub"), None),
        P(("groups", "region", "sub"), None),
        P(("groups", "region", "sub"), None),
        P(),
        P(),
        P(),
        P(),
        P(),
        P(),
        P(),
        P(),
        P(),
        P(),
        P(("groups", "region", "sub"), None, None),
        P(("groups", "region", "sub")),
        P(("groups", "region", "sub")),
        P("groups"),
        P("groups"),
    )
    out_specs = (
        P(("groups", "region", "sub"), None),
        P(("groups", "region", "sub"), None),
        P(("groups", "region", "sub"), None),
        P(("groups", "region", "sub"), None),
        P(("groups", "region", "sub"), None),
        P(("groups", "region", "sub"), None),
        P(("groups", "region", "sub"), None),
    )
    small = mesh.shape["region"] == SIDE and mesh.shape["sub"] == SIDE
    return jax.shard_map(
        fused_device if small else per_device, mesh=mesh, in_specs=in_specs, out_specs=out_specs, check_vma=False
    )
```
